256 devices in a mesh: freq: 8 (over y_lo, x), ma: 32 (over z, y_hi, core).
Axes of the slice: x: 4, y: 4 (y_hi: 2, y_lo: 2; y = y_hi * 2 + y_lo), z: 8, core: 2. Of those that a mesh axis runs over, the one named last changes fastest.
Arguments:
- visibility: bfloat16 [8, 2048, 2, 1024], P('freq', 'ma'), may hold values from -6 to 6
- beam_blocks: bfloat16 [8, 64, 2, 1024, 1024], P('freq', 'ma'), may hold values from -0.1875 to 0.1875
- legendre: bfloat16 [64, 1024, 1024], P('ma'), may hold values from -0.1875 to 0.1875
- m_table: int32 [64], replicated, may hold values from 0 to 63, each once
- mode_counts: int32 [64], replicated, may hold values from 256 to 1024, as said below
- moment_weights: float32 [3, 8], replicated, may hold values from -2 to 2
Outputs:
- moments: float32 [3, 1024, 2048], P(None, 'ma', 'freq')
The draws below stay inside these ranges and needn't reach their ends.
Inputs may be any that keep to these rules, and one draw needn't show every extreme that they name: `m_table`: each m of 0 to 63 stands in exactly one slot. `mode_counts`: m = 0 keeps all 1024 modes.
All inputs are finite; a program needn't handle non-finite values.
Results may differ from the reference program's by a relative error of at most 0.0041.
Values may be sent and summed in bfloat16 or wider, within the bound.
No kernel may reach another device: no remote copies, remote signals or barrier semaphores. Data moves between devices by JAX's collectives and lax.ppermute only.
A program may use at most 64 MiB of HBM per device.

```python
import math
import jax
import jax.numpy as jnp
from jax import lax

B = 1024
L = 1024
NT = 2048
NPHI = 2048
NMOM = 3
F = 8
M = 64
R = 1024


def draw_mode_counts(key, part):
    key = jax.random.fold_in(key, 23)
    order = jnp.arange(M, dtype=jnp.int32)
    floor_count = B // 4
    slope = (M - 1 - order) * (B - floor_count) // max(M - 1, 1)
    jitter = jax.random.randint(key, (M,), 0, max(B // 16, 1), dtype=jnp.int32)
    jitter = jnp.where((order == 0) | (order == M - 1), 0, jitter)
    counts = jnp.maximum(floor_count + slope - jitter, floor_count)
    return counts.astype(jnp.int32)


def shard_levels(own_key, shape, pieces, low, high):
    factor_of = 1.0
    for position, parts in pieces:
        steps = jax.random.uniform(jax.random.fold_in(jax.random.fold_in(own_key, 6), position), (parts,), jnp.float32, low / len(pieces), high / len(pieces))
        factor_of = factor_of * jnp.repeat(jnp.exp(steps), shape[position] // parts).reshape((-1,) + (1,) * (len(shape) - 1 - position))
    return factor_of


def centred(rng, extent, scale, limit, pieces=(), kind=jnp.bfloat16):
    factor_of = shard_levels(rng, extent, pieces, -0.22, 0.18) if pieces else 1.0
    values = jax.random.normal(rng, extent, jnp.float32) * scale * factor_of
    return jnp.minimum(jnp.maximum(values, -limit), limit).astype(kind)


def setup_inputs(seed: int = 0) -> dict:
    keys = jax.random.split(jax.random.key(seed), 7)
    return {
        "visibility": centred(keys[0], (F, NT, 2, B), 1.0, 6.0, ((0, 8), (1, 32))),
        "beam_blocks": centred(keys[1], (F, M, 2, B, L), B ** -0.5, 0.1875, ((0, 8), (1, 32))),
        "legendre": centred(keys[2], (M, L, R), L ** -0.5, 0.1875, ((0, 32),)),
        "m_table": jax.random.permutation(keys[3], M).astype(jnp.int32),
        "mode_counts": draw_mode_counts(jax.random.fold_in(keys[6], 71), 0),
        "moment_weights": centred(keys[5], (NMOM, F), F ** -0.5, 2.0, (), jnp.float32),
    }


highest = lax.Precision.HIGHEST

def slot_counts(m_table, mode_counts):
    matches = m_table[:, None] == jnp.arange(mode_counts.shape[0], dtype=jnp.int32)[None, :]
    return lax.optimization_barrier(jnp.sum(jnp.where(matches, mode_counts[None, :], 0), axis=1)).astype(jnp.int32)

def along_time(table, data):
    return jnp.einsum('mt,ftb->mfb', table, data, precision=highest)

def reference(visibility, beam_blocks, legendre, m_table, mode_counts, moment_weights):
    times = jnp.arange(NT, dtype=jnp.int32)
    phase_index = m_table[:, None] * times[None, :] % NT
    angles = phase_index.astype(jnp.float32) * jnp.float32(2.0 * math.pi / NT)
    cosine = jnp.cos(angles)
    sine_part = jnp.sin(angles)
    values = visibility.astype(jnp.float32)
    real_vis = values[:, :, 0, :]
    imag_vis = values[:, :, 1, :]
    norm_factor = jnp.float32(1.0 / math.sqrt(NT))
    real_spec = (along_time(cosine, real_vis) + along_time(sine_part, imag_vis)) * norm_factor
    imag_spec = (along_time(cosine, imag_vis) - along_time(sine_part, real_vis)) * norm_factor
    per_slot = slot_counts(m_table, mode_counts)
    keep_mask = (jnp.arange(B, dtype=jnp.int32)[None, :] < per_slot[:, None]).astype(jnp.float32)
    spectra = (jnp.stack([real_spec, imag_spec], axis=2) * keep_mask[:, None, None, :]).astype(jnp.bfloat16)

    def one_slot(slot):
        block = lax.dynamic_index_in_dim(beam_blocks, slot, 1, keepdims=False).astype(jnp.float32)
        spec_slot = lax.dynamic_index_in_dim(spectra, slot, 0, keepdims=False).astype(jnp.float32)
        products = jnp.einsum('fcb,fdbl->fcdl', spec_slot, block)
        real_part = products[:, 0, 0] + products[:, 1, 1]
        imag_part = products[:, 1, 0] - products[:, 0, 1]
        m_value = lax.dynamic_index_in_dim(m_table, slot, 0, keepdims=False)
        l_mask = (jnp.arange(L, dtype=jnp.int32) >= m_value).astype(jnp.float32)
        coeffs = (jnp.stack([real_part, imag_part], axis=1) * l_mask[None, None, :]).astype(jnp.bfloat16)
        table = lax.dynamic_index_in_dim(legendre, slot, 0, keepdims=False).astype(jnp.float32)
        return jnp.einsum('fcl,lr->fcr', coeffs.astype(jnp.float32), table)
    cycle_coeffs = lax.map(one_slot, jnp.arange(M, dtype=jnp.int32))
    pixels = jnp.arange(NPHI, dtype=jnp.int32)
    pixel_index = m_table[:, None] * pixels[None, :] % NPHI
    pixel_angles = pixel_index.astype(jnp.float32) * jnp.float32(2.0 * math.pi / NPHI)
    weights_m = jnp.where(m_table == 0, 1.0, 2.0).astype(jnp.float32) * jnp.float32(1.0 / math.sqrt(2 * M))
    cos_weighted = jnp.cos(pixel_angles) * weights_m[:, None]
    sin_weighted = jnp.sin(pixel_angles) * weights_m[:, None]
    cycle_maps = jnp.einsum('mfr,mp->frp', cycle_coeffs[:, :, 0], cos_weighted, precision=highest) - jnp.einsum('mfr,mp->frp', cycle_coeffs[:, :, 1], sin_weighted, precision=highest)
    return jnp.einsum('kf,frp->krp', moment_weights, cycle_maps, precision=highest)
```

```python
import functools
import math

import jax
import jax.numpy as jnp
from jax import lax
from jax.experimental import pallas as pl
from jax.experimental.pallas import tpu as pltpu
from jax.sharding import PartitionSpec as P

f32, bf16, i32 = jnp.float32, jnp.bfloat16, jnp.int32
CIRCLE = 2048
VMEM = pl.BlockSpec(memory_space=pltpu.VMEM)
SMEM = pl.BlockSpec(memory_space=pltpu.SMEM)


def iota(shape, dim):
    return lax.broadcasted_iota(i32, shape, dim)


def cos_of_index(index):
    folded = jnp.abs((index & (CIRCLE - 1)) - CIRCLE // 2) - CIRCLE // 4
    x = folded.astype(f32) * f32(2.0 * math.pi / CIRCLE)
    y = x * x
    poly = f32(1.0 / math.factorial(13))
    for n in (11, 9, 7, 5, 3):
        poly = poly * y + f32((-1.0) ** (n // 2) / math.factorial(n))
    return x + x * y * poly


def select_m(m_ref, slots):
    lanes = iota((slots.shape[0], m_ref.shape[1]), 1)
    return jnp.sum(jnp.where(lanes == slots, m_ref[...], 0).astype(f32), axis=1, keepdims=True).astype(i32)


def split(x):
    high = x.astype(bf16)
    return high, (x - high.astype(f32)).astype(bf16)


def time_table_kernel(m_ref, table_ref, *, time_local):
    place = lax.axis_index("ma")
    rows, columns = table_ref.shape[0] // 2, table_ref.shape[1] // 2
    m_rows = select_m(m_ref, iota((rows, 1), 0) >> 1)
    out_part = iota((rows, columns), 0) & 1
    column = iota((rows, columns), 1)
    quarter = ((column & 1) - out_part) * (CIRCLE // 4)
    for other in range(2):
        first = (place ^ other) * time_local
        values = cos_of_index(m_rows * (first + (column >> 1)) - quarter)
        high, low = split(values)
        where = slice(other * columns, (other + 1) * columns)
        table_ref[:rows, where] = high
        table_ref[rows:, where] = low


def transform_kernel(table_ref, own_ref, other_ref, out_ref):
    half = out_ref.shape[1]
    first = pl.multiple_of((lax.axis_index("ma") & 1) * half, half)
    depth = own_ref.shape[0]
    total = jnp.dot(
        table_ref[:, :depth], own_ref[:, pl.ds(first, half)], preferred_element_type=f32
    ) + jnp.dot(
        table_ref[:, depth:], other_ref[:, pl.ds(first, half)], preferred_element_type=f32
    )
    rows = out_ref.shape[0]
    out_ref[...] = total[:rows] + total[rows:]


def contract_kernel(m_ref, count_ref, parts_ref, beam_ref, legendre_ref, out_ref, sums, *, norm):
    place = lax.axis_index("ma")
    sources = parts_ref.shape[0]
    halves = []
    for core in range(2):
        total = parts_ref[core]
        for source in range(core + 2, sources, 2):
            total = total + parts_ref[source]
        halves.append(total)
    spectra = jnp.concatenate(halves, axis=1) * f32(norm)
    slots = beam_ref.shape[0]
    modes, degrees = beam_ref.shape[2:]
    cycles = legendre_ref.shape[2]
    m_own = [m_ref[place * slots + j] for j in range(slots)]
    row = iota(spectra.shape, 0)
    counts = jnp.zeros(spectra.shape, i32)
    for j in range(slots):
        counts = jnp.where(row >> 1 == j, count_ref[m_own[j]], counts)
    spectra = jnp.where(iota(spectra.shape, 1) < counts, spectra, 0.0).astype(bf16)
    for j in range(slots):
        with_real = jnp.dot(spectra, beam_ref[j, 0], preferred_element_type=f32)
        with_imag = jnp.dot(spectra, beam_ref[j, 1], preferred_element_type=f32)
        re, im = 2 * j, 2 * j + 1
        coeffs = jnp.concatenate(
            [
                with_real[re : re + 1] + with_imag[im : im + 1],
                with_real[im : im + 1] - with_imag[re : re + 1],
            ],
            axis=0,
        )
        coeffs = jnp.where(iota(coeffs.shape, 1) >= m_own[j], coeffs, 0.0).astype(bf16)
        cycle = jnp.dot(coeffs, legendre_ref[j], preferred_element_type=f32)
        for c in range(2):
            for g in range(cycles // 128):
                sums[2 * j + c, pl.ds(g, 1), :] = cycle[c : c + 1, g * 128 : (g + 1) * 128]
    block = iota((cycles // 128, 128), 1) >> 5
    copies = out_ref.shape[0] // (cycles // 32)
    for a in range(4):
        value = sums[0] if a == 0 else pltpu.roll(sums[0], 128 - 32 * a, 1)
        for q in range(1, 4):
            moved = sums[q] if a == q else pltpu.roll(sums[q], (32 * (q - a)) % 128, 1)
            value = jnp.where(block == q, moved, value)
        for f in range(copies):
            out_ref[pl.ds(f * (cycles // 32) + a, cycles // 128, stride=4), :] = value


def azimuth_kernel(m_ref, table_ref):
    rows, pixels = table_ref.shape
    row = iota((rows, 1), 0)
    m_rows = select_m(m_ref, 2 * (row & 31) + (row >> 6))
    weights = jnp.where(m_rows == 0, 1.0, 2.0).astype(f32) * f32(1.0 / math.sqrt(rows))
    first = lax.axis_index("freq") * pixels
    index = m_rows * (first + iota((rows, pixels), 1)) + ((row >> 5) & 1) * (CIRCLE // 4)
    table_ref[...] = cos_of_index(index) * weights


def synthesis_kernel(weight_ref, sums_ref, table_ref, out_ref):
    moments, cycles, _ = out_ref.shape
    freqs = weight_ref.shape[1]
    owners = sums_ref.shape[0] // freqs
    blocks = [sums_ref[f * owners : (f + 1) * owners, :] for f in range(freqs)]
    turned = []
    for k in range(moments):
        total = weight_ref[k, 0] * blocks[0]
        for f in range(1, freqs):
            total = total + weight_ref[k, f] * blocks[f]
        flipped = total.T
        turned.append(
            jnp.concatenate([flipped[q * cycles : (q + 1) * cycles] for q in range(4)], axis=1)
        )
    out = jnp.dot(
        jnp.concatenate(turned, axis=0),
        table_ref[...],
        precision=lax.Precision.HIGHEST,
        preferred_element_type=f32,
    )
    for k in range(moments):
        out_ref[k] = out[k * cycles : (k + 1) * cycles]


def params(mib):
    return pltpu.CompilerParams(vmem_limit_bytes=mib << 20)


def local(visibility, beam_blocks, legendre, m_table, mode_counts, moment_weights):
    time_local, modes = visibility.shape[1], visibility.shape[3]
    places = lax.axis_size("ma")
    freqs = lax.axis_size("freq")
    total_time = time_local * places
    slots_all = m_table.shape[0]
    slots = slots_all // places
    cycles = legendre.shape[2]
    moments = moment_weights.shape[0]
    depth = 2 * time_local
    m_line = m_table[None, :]

    other = lax.ppermute(visibility, "ma", [(i, i ^ 1) for i in range(places)])
    table = pl.pallas_call(
        functools.partial(time_table_kernel, time_local=time_local),
        out_shape=jax.ShapeDtypeStruct((4 * slots_all, 2 * depth), bf16),
        in_specs=[VMEM],
        out_specs=VMEM,
        compiler_params=params(16),
        name="time_table",
    )(m_line)
    parts = pl.pallas_call(
        transform_kernel,
        out_shape=jax.ShapeDtypeStruct((2 * slots_all, modes // 2), f32),
        in_specs=[VMEM, VMEM, VMEM],
        out_specs=VMEM,
        compiler_params=params(16),
        name="transform",
    )(table, visibility.reshape(depth, modes), other.reshape(depth, modes))
    parts = lax.all_to_all(
        parts.reshape(places, 2 * slots, modes // 2), "ma", split_axis=0, concat_axis=0
    )
    sums = pl.pallas_call(
        functools.partial(contract_kernel, norm=1.0 / math.sqrt(total_time)),
        out_shape=jax.ShapeDtypeStruct((freqs * places, 128), f32),
        in_specs=[SMEM, SMEM, VMEM, VMEM, VMEM],
        out_specs=VMEM,
        scratch_shapes=[pltpu.VMEM((2 * slots, cycles // 128, 128), f32)],
        compiler_params=params(48),
        name="contract",
    )(m_table, mode_counts, parts, beam_blocks[0], legendre)
    sums = lax.all_to_all(
        sums[:, None, :], ("freq", "ma"), split_axis=0, concat_axis=0
    ).reshape(freqs * places, 128)
    azimuth = pl.pallas_call(
        azimuth_kernel,
        out_shape=jax.ShapeDtypeStruct((2 * slots_all, CIRCLE // freqs), f32),
        in_specs=[VMEM],
        out_specs=VMEM,
        compiler_params=params(16),
        name="azimuth",
    )(m_line)
    return pl.pallas_call(
        synthesis_kernel,
        out_shape=jax.ShapeDtypeStruct((moments, cycles // places, CIRCLE // freqs), f32),
        in_specs=[SMEM, VMEM, VMEM],
        out_specs=VMEM,
        compiler_params=params(16),
        name="synthesis",
    )(moment_weights, sums, azimuth)


def solution(mesh):
    placed = (
        P("freq", "ma", None, None),
        P("freq", "ma", None, None, None),
        P("ma", None, None),
        P(),
        P(),
        P(),
    )
    return jax.shard_map(
        local, mesh=mesh, in_specs=placed, out_specs=P(None, "ma", "freq"), check_vma=False
    )
```

```python
import functools
import math

import jax
import jax.numpy as jnp
from jax import lax
from jax.experimental import pallas as pl
from jax.experimental.pallas import tpu as pltpu
from jax.sharding import PartitionSpec as P

f32, bf16, i32 = jnp.float32, jnp.bfloat16, jnp.int32
PIECES = 2
HEADS = 2
CIRCLE = 2048
VMEM = pl.BlockSpec(memory_space=pltpu.VMEM)
ANY = pl.BlockSpec(memory_space=pl.ANY)
SMEM = pl.BlockSpec(memory_space=pltpu.SMEM)


def iota(shape, dim):
    return lax.broadcasted_iota(i32, shape, dim)


def cos_of_index(index):
    folded = jnp.abs((index & (CIRCLE - 1)) - CIRCLE // 2) - CIRCLE // 4
    x = folded.astype(f32) * f32(2.0 * math.pi / CIRCLE)
    y = x * x
    poly = f32(1.0 / math.factorial(13))
    for n in (11, 9, 7, 5, 3):
        poly = poly * y + f32((-1.0) ** (n // 2) / math.factorial(n))
    return x + x * y * poly


def select_m(m_ref, slots):
    lanes = iota((slots.shape[0], m_ref.shape[1]), 1)
    return jnp.sum(jnp.where(lanes == slots, m_ref[...], 0).astype(f32), axis=1, keepdims=True).astype(i32)


def split(x):
    high = x.astype(bf16)
    return high, (x - high.astype(f32)).astype(bf16)


def time_table(m_ref, table_ref, time_local):
    place = lax.axis_index("ma")
    rows, columns = table_ref.shape[0] // 2, table_ref.shape[1] // 2
    m_rows = select_m(m_ref, iota((rows, 1), 0) >> 1)
    out_part = iota((rows, columns), 0) & 1
    column = iota((rows, columns), 1)
    quarter = ((column & 1) - out_part) * (CIRCLE // 4)
    for other in range(2):
        first = (place ^ other) * time_local
        values = cos_of_index(m_rows * (first + (column >> 1)) - quarter)
        high, low = split(values)
        where = slice(other * columns, (other + 1) * columns)
        table_ref[:rows, where] = high
        table_ref[rows:, where] = low


def transform_kernel(table_ref, own_ref, other_ref, out_ref):
    half = out_ref.shape[1]
    first = pl.multiple_of((lax.axis_index("ma") & 1) * half, half)
    depth = own_ref.shape[0]
    total = jnp.dot(
        table_ref[:, :depth], own_ref[:, pl.ds(first, half)], preferred_element_type=f32
    ) + jnp.dot(
        table_ref[:, depth:], other_ref[:, pl.ds(first, half)], preferred_element_type=f32
    )
    rows = out_ref.shape[0]
    out_ref[...] = total[:rows] + total[rows:]


def prepare_kernel(
    m_ref, count_ref, weight_ref, m_line_ref, beam_hbm,
    head_ref, mode_ref, degree_ref, azimuth_ref, table_ref, spread_ref, sems, *, norm, time_local
):
    copies = [
        pltpu.make_async_copy(
            beam_hbm.at[j // PIECES, pl.ds(j % PIECES * head_ref.shape[1], head_ref.shape[1])],
            head_ref.at[j],
            sems.at[j],
        )
        for j in range(head_ref.shape[0])
    ]
    for copy in copies:
        copy.start()
    time_table(m_line_ref, table_ref, time_local)
    place = lax.axis_index("ma")
    slots = mode_ref.shape[0] // 2
    m_own = [m_ref[place * slots + j] for j in range(slots)]
    shape = mode_ref.shape
    counts = jnp.zeros(shape, i32)
    for j in range(slots):
        counts = jnp.where(iota(shape, 0) >> 1 == j, count_ref[m_own[j]], counts)
    mode_ref[...] = jnp.where(iota(shape, 1) < counts, f32(norm), f32(0.0))
    shape = degree_ref.shape
    firsts = jnp.zeros(shape, i32)
    for j in range(slots):
        firsts = jnp.where(iota(shape, 0) >> 1 == j, m_own[j], firsts)
    degree_ref[...] = jnp.where(iota(shape, 1) >= firsts, f32(1.0), f32(0.0))

    rows, pixels = azimuth_ref.shape[1:]
    row = iota((rows, 1), 0)
    m_rows = select_m(m_line_ref, 2 * (row & 31) + (row >> 6))
    weights = jnp.where(m_rows == 0, 1.0, 2.0).astype(f32) * f32(1.0 / math.sqrt(rows))
    first = lax.axis_index("freq") * pixels
    index = m_rows * (first + iota((rows, pixels), 1)) + ((row >> 5) & 1) * (CIRCLE // 4)
    azimuth_ref[0], azimuth_ref[1] = split(cos_of_index(index) * weights)
    for k in range(weight_ref.shape[0]):
        for f in range(weight_ref.shape[1]):
            spread_ref[k, f : f + 1, :] = jnp.full((1, 128), weight_ref[k, f], f32)
    for copy in copies:
        copy.wait()


def contract_kernel(
    parts_ref, mode_ref, degree_ref, head_ref, beam_hbm, legendre_hbm, out_ref, sums, beam, legendre, sems
):
    heads, rows = head_ref.shape[:2]
    slots = legendre_hbm.shape[0]
    pieces = [
        (source, target, j, part)
        for source, target, blocks in ((beam_hbm, beam, 2 * slots), (legendre_hbm, legendre, slots))
        for j in range(blocks)
        for part in range(PIECES)
    ][heads:]
    copies = {}
    for n, (source, target, j, part) in enumerate(pieces):
        place = pl.ds(part * rows, rows)
        copies[target is legendre, j, part] = copy = pltpu.make_async_copy(
            source.at[j, place], target.at[j, place], sems.at[n]
        )
        copy.start()

    def product(left, right, is_legendre, j):
        total = None
        for part in range(PIECES):
            place = slice(part * rows, (part + 1) * rows)
            if (is_legendre, j, part) in copies:
                copies[is_legendre, j, part].wait()
                block = right[j, place, :]
            else:
                block = head_ref[j * PIECES + part]
            term = jnp.dot(left[:, place], block, preferred_element_type=f32)
            total = term if total is None else total + term
        return total

    halves = []
    for core in range(2):
        total = parts_ref[core]
        for source in range(core + 2, parts_ref.shape[0], 2):
            total = total + parts_ref[source]
        halves.append(total)
    spectra = (jnp.concatenate(halves, axis=1) * mode_ref[...]).astype(bf16)
    coeffs = []
    for j in range(slots):
        with_real = product(spectra, beam, False, 2 * j)
        with_imag = product(spectra, beam, False, 2 * j + 1)
        re, im = 2 * j, 2 * j + 1
        both = jnp.concatenate(
            [
                with_real[re : re + 1] + with_imag[im : im + 1],
                with_real[im : im + 1] - with_imag[re : re + 1],
            ],
            axis=0,
        )
        coeffs.append((both * degree_ref[re : re + 2, :]).astype(bf16))
    cycles = legendre.shape[2]
    for j in range(slots):
        cycle = product(coeffs[j], legendre, True, j)
        for c in range(2):
            for g in range(cycles // 128):
                sums[2 * j + c, pl.ds(g, 1), :] = cycle[c : c + 1, g * 128 : (g + 1) * 128]
    block = iota((cycles // 128, 128), 1) >> 5
    copies = out_ref.shape[0] // (cycles // 32)
    for a in range(4):
        value = sums[0] if a == 0 else pltpu.roll(sums[0], 128 - 32 * a, 1)
        for q in range(1, 4):
            moved = sums[q] if a == q else pltpu.roll(sums[q], (32 * (q - a)) % 128, 1)
            value = jnp.where(block == q, moved, value)
        for f in range(copies):
            out_ref[pl.ds(f * (cycles // 32) + a, cycles // 128, stride=4), :] = value


def synthesis_kernel(spread_ref, sums_ref, azimuth_ref, out_ref):
    moments, cycles, _ = out_ref.shape
    freqs = spread_ref.shape[1]
    owners = sums_ref.shape[0] // freqs
    blocks = [sums_ref[f * owners : (f + 1) * owners, :] for f in range(freqs)]
    turned = []
    for k in range(moments):
        total = spread_ref[k, 0:1, :] * blocks[0]
        for f in range(1, freqs):
            total = total + spread_ref[k, f : f + 1, :] * blocks[f]
        flipped = total.T
        turned.append(
            jnp.concatenate([flipped[q * cycles : (q + 1) * cycles] for q in range(4)], axis=1)
        )
    high, low = split(jnp.concatenate(turned, axis=0))
    out = (
        jnp.dot(high, azimuth_ref[0], preferred_element_type=f32)
        + jnp.dot(high, azimuth_ref[1], preferred_element_type=f32)
        + jnp.dot(low, azimuth_ref[0], preferred_element_type=f32)
    )
    for k in range(moments):
        out_ref[k] = out[k * cycles : (k + 1) * cycles]


def params(mib):
    return pltpu.CompilerParams(vmem_limit_bytes=mib << 20)


def local(visibility, beam_blocks, legendre, m_table, mode_counts, moment_weights):
    time_local, modes = visibility.shape[1], visibility.shape[3]
    places = lax.axis_size("ma")
    freqs = lax.axis_size("freq")
    total_time = time_local * places
    slots_all = m_table.shape[0]
    slots = slots_all // places
    cycles = legendre.shape[2]
    moments = moment_weights.shape[0]
    depth = 2 * time_local

    other = lax.ppermute(visibility, "ma", [(i, i ^ 1) for i in range(places)])
    beam, degrees = beam_blocks.reshape(2 * slots, modes, -1), beam_blocks.shape[4]
    rows = modes // PIECES
    head, mode_mask, degree_mask, azimuth, table, spread = pl.pallas_call(
        functools.partial(prepare_kernel, norm=1.0 / math.sqrt(total_time), time_local=time_local),
        out_shape=(
            pltpu.VMEM((HEADS, rows, degrees), bf16),
            pltpu.VMEM((2 * slots, modes), f32),
            pltpu.VMEM((2 * slots, degrees), f32),
            pltpu.VMEM((2, 2 * slots_all, CIRCLE // freqs), bf16),
            pltpu.VMEM((4 * slots_all, 2 * depth), bf16),
            pltpu.VMEM((moments, freqs, 128), f32),
        ),
        in_specs=[SMEM, SMEM, SMEM, VMEM, ANY],
        out_specs=(VMEM,) * 6,
        scratch_shapes=[pltpu.SemaphoreType.DMA((HEADS,))],
        compiler_params=params(54),
        name="prepare",
    )(m_table, mode_counts, moment_weights, m_table[None, :], beam)
    parts = pl.pallas_call(
        transform_kernel,
        out_shape=jax.ShapeDtypeStruct((2 * slots_all, modes // 2), f32),
        in_specs=[VMEM, VMEM, VMEM],
        out_specs=VMEM,
        compiler_params=params(16),
        name="transform",
    )(table, visibility.reshape(depth, modes), other.reshape(depth, modes))
    parts = lax.all_to_all(
        parts.reshape(places, 2 * slots, modes // 2), "ma", split_axis=0, concat_axis=0
    )
    sums = pl.pallas_call(
        contract_kernel,
        out_shape=pltpu.VMEM((freqs * places, 128), f32),
        in_specs=[VMEM, VMEM, VMEM, VMEM, ANY, ANY],
        out_specs=VMEM,
        scratch_shapes=[
            pltpu.VMEM((2 * slots, cycles // 128, 128), f32),
            pltpu.VMEM(beam.shape, bf16),
            pltpu.VMEM(legendre.shape, bf16),
            pltpu.SemaphoreType.DMA((3 * slots * PIECES - HEADS,)),
        ],
        compiler_params=params(48),
        name="contract",
    )(parts, mode_mask, degree_mask, head, beam, legendre)
    sums = lax.all_to_all(
        sums[:, None, :], ("freq", "ma"), split_axis=0, concat_axis=0
    ).reshape(freqs * places, 128)
    return pl.pallas_call(
        synthesis_kernel,
        out_shape=jax.ShapeDtypeStruct((moments, cycles // places, CIRCLE // freqs), f32),
        in_specs=[VMEM, VMEM, VMEM],
        out_specs=VMEM,
        compiler_params=params(16),
        name="synthesis",
    )(spread, sums, azimuth)


def solution(mesh):
    placed = (
        P("freq", "ma", None, None),
        P("freq", "ma", None, None, None),
        P("ma", None, None),
        P(),
        P(),
        P(),
    )
    return jax.shard_map(
        local, mesh=mesh, in_specs=placed, out_specs=P(None, "ma", "freq"), check_vma=False
    )
```

```python
import functools
import math

import jax
import jax.numpy as jnp
from jax import lax
from jax.experimental import pallas as pl
from jax.experimental.pallas import tpu as pltpu
from jax.sharding import PartitionSpec as P

f32, bf16, i32 = jnp.float32, jnp.bfloat16, jnp.int32
PIECES = 4
HEADS = 4
CIRCLE = 2048
VMEM = pl.BlockSpec(memory_space=pltpu.VMEM)
ANY = pl.BlockSpec(memory_space=pl.ANY)
SMEM = pl.BlockSpec(memory_space=pltpu.SMEM)


def iota(shape, dim):
    return lax.broadcasted_iota(i32, shape, dim)


def cos_of_index(index):
    folded = jnp.abs((index & (CIRCLE - 1)) - CIRCLE // 2) - CIRCLE // 4
    x = folded.astype(f32) * f32(2.0 * math.pi / CIRCLE)
    y = x * x
    poly = f32(1.0 / math.factorial(13))
    for n in (11, 9, 7, 5, 3):
        poly = poly * y + f32((-1.0) ** (n // 2) / math.factorial(n))
    return x + x * y * poly


def select_m(m_ref, slots):
    lanes = iota((slots.shape[0], m_ref.shape[1]), 1)
    return jnp.sum(jnp.where(lanes == slots, m_ref[...], 0).astype(f32), axis=1, keepdims=True).astype(i32)


def split(x):
    high = x.astype(bf16)
    return high, (x - high.astype(f32)).astype(bf16)


def time_table(m_ref, table_ref, time_local):
    place = lax.axis_index("ma")
    rows, columns = table_ref.shape[0] // 2, table_ref.shape[1] // 2
    m_rows = select_m(m_ref, iota((rows, 1), 0) >> 1)
    out_part = iota((rows, columns), 0) & 1
    column = iota((rows, columns), 1)
    quarter = ((column & 1) - out_part) * (CIRCLE // 4)
    for other in range(2):
        first = (place ^ other) * time_local
        values = cos_of_index(m_rows * (first + (column >> 1)) - quarter)
        high, low = split(values)
        where = slice(other * columns, (other + 1) * columns)
        table_ref[:rows, where] = high
        table_ref[rows:, where] = low


def transform_kernel(table_ref, own_ref, other_ref, out_ref):
    half = out_ref.shape[1]
    first = pl.multiple_of((lax.axis_index("ma") & 1) * half, half)
    depth = own_ref.shape[0]
    total = jnp.dot(
        table_ref[:, :depth], own_ref[:, pl.ds(first, half)], preferred_element_type=f32
    ) + jnp.dot(
        table_ref[:, depth:], other_ref[:, pl.ds(first, half)], preferred_element_type=f32
    )
    rows = out_ref.shape[0]
    out_ref[...] = total[:rows] + total[rows:]


def prepare_kernel(
    m_hbm, count_hbm, weight_hbm, m_line_hbm, own_hbm, beam_hbm,
    head_ref, own_ref, mode_ref, degree_ref, table_ref, spread_ref, line_ref,
    m_ref, count_ref, weight_ref, own, small_sems, sems, *, norm, time_local
):
    small = [
        pltpu.make_async_copy(source, target, small_sems.at[n])
        for n, (source, target) in enumerate(
            (
                (m_line_hbm, line_ref),
                (own_hbm, own),
                (m_hbm, m_ref),
                (count_hbm, count_ref),
                (weight_hbm, weight_ref),
            )
        )
    ]
    rows = head_ref.shape[1]
    heads = [
        pltpu.make_async_copy(
            beam_hbm.at[j // PIECES, pl.ds(j % PIECES * rows, rows)], head_ref.at[j], sems.at[j]
        )
        for j in range(head_ref.shape[0])
    ]
    for copy in small + heads:
        copy.start()
    small[0].wait()
    time_table(line_ref, table_ref, time_local)
    small[1].wait()
    own_ref[...] = own[...].reshape(own_ref.shape)
    for copy in small[2:]:
        copy.wait()
    place = lax.axis_index("ma")
    slots = mode_ref.shape[0] // 2
    m_own = [m_ref[place * slots + j] for j in range(slots)]
    shape = mode_ref.shape
    counts = jnp.zeros(shape, i32)
    for j in range(slots):
        counts = jnp.where(iota(shape, 0) >> 1 == j, count_ref[m_own[j]], counts)
    mode_ref[...] = jnp.where(iota(shape, 1) < counts, f32(norm), f32(0.0))
    shape = degree_ref.shape
    firsts = jnp.zeros(shape, i32)
    for j in range(slots):
        firsts = jnp.where(iota(shape, 0) >> 1 == j, m_own[j], firsts)
    degree_ref[...] = jnp.where(iota(shape, 1) >= firsts, f32(1.0), f32(0.0))
    for k in range(weight_ref.shape[0]):
        for f in range(weight_ref.shape[1]):
            spread_ref[k, f : f + 1, :] = jnp.full((1, 128), weight_ref[k, f], f32)
    for copy in heads:
        copy.wait()


def azimuth_table(m_ref, table_ref):
    rows, pixels = table_ref.shape[1:]
    row = iota((rows, 1), 0)
    m_rows = select_m(m_ref, 2 * (row & 31) + (row >> 6))
    weights = jnp.where(m_rows == 0, 1.0, 2.0).astype(f32) * f32(1.0 / math.sqrt(rows))
    first = lax.axis_index("freq") * pixels
    index = m_rows * (first + iota((rows, pixels), 1)) + ((row >> 5) & 1) * (CIRCLE // 4)
    table_ref[0], table_ref[1] = split(cos_of_index(index) * weights)


def contract_kernel(
    parts_ref, mode_ref, degree_ref, line_ref, head_ref, beam_hbm, legendre_hbm,
    out_ref, azimuth_ref, sums, beam, legendre, sems
):
    heads, rows = head_ref.shape[:2]
    slots = legendre_hbm.shape[0]
    pieces = [
        (False, 2 * j + d, part) for j in range(slots) for d in range(2) for part in range(PIECES)
    ][heads:]
    for j in range(slots):
        after = [n for n, piece in enumerate(pieces) if not piece[0] and piece[1] < 2 * (j + 1)]
        pieces[after[-1] + 1 : after[-1] + 1] = [(True, j, part) for part in range(PIECES)]
    copies = {}
    for n, piece in enumerate(pieces):
        is_legendre, j, part = piece
        source, target = (legendre_hbm, legendre) if is_legendre else (beam_hbm, beam)
        place = pl.ds(part * rows, rows)
        copies[piece] = pltpu.make_async_copy(source.at[j, place], target.at[j, place], sems.at[n])
        copies[piece].start()
    azimuth_table(line_ref, azimuth_ref)

    def product(left, is_legendre, j):
        total = None
        for part in range(PIECES):
            place = slice(part * rows, (part + 1) * rows)
            piece = (is_legendre, j, part)
            if piece in copies:
                copies[piece].wait()
                block = (legendre if is_legendre else beam)[j, place, :]
            else:
                block = head_ref[j * PIECES + part]
            term = jnp.dot(left[:, place], block, preferred_element_type=f32)
            total = term if total is None else total + term
        return total

    halves = []
    for core in range(2):
        total = parts_ref[core]
        for source in range(core + 2, parts_ref.shape[0], 2):
            total = total + parts_ref[source]
        halves.append(total)
    spectra = (jnp.concatenate(halves, axis=1) * mode_ref[...]).astype(bf16)
    cycles = legendre.shape[2]
    for j in range(slots):
        with_real = product(spectra, False, 2 * j)
        with_imag = product(spectra, False, 2 * j + 1)
        re, im = 2 * j, 2 * j + 1
        coeffs = jnp.concatenate(
            [
                with_real[re : re + 1] + with_imag[im : im + 1],
                with_real[im : im + 1] - with_imag[re : re + 1],
            ],
            axis=0,
        )
        cycle = product((coeffs * degree_ref[re : re + 2, :]).astype(bf16), True, j)
        for c in range(2):
            for g in range(cycles // 128):
                sums[2 * j + c, pl.ds(g, 1), :] = cycle[c : c + 1, g * 128 : (g + 1) * 128]
    block = iota((cycles // 128, 128), 1) >> 5
    copies = out_ref.shape[0] // (cycles // 32)
    for a in range(4):
        value = sums[0] if a == 0 else pltpu.roll(sums[0], 128 - 32 * a, 1)
        for q in range(1, 4):
            moved = sums[q] if a == q else pltpu.roll(sums[q], (32 * (q - a)) % 128, 1)
            value = jnp.where(block == q, moved, value)
        for f in range(copies):
            out_ref[pl.ds(f * (cycles // 32) + a, cycles // 128, stride=4), :] = value


def synthesis_kernel(spread_ref, sums_ref, azimuth_ref, out_ref):
    moments, cycles, _ = out_ref.shape
    freqs = spread_ref.shape[1]
    owners = sums_ref.shape[0] // freqs
    blocks = [sums_ref[f * owners : (f + 1) * owners, :] for f in range(freqs)]
    turned = []
    for k in range(moments):
        total = spread_ref[k, 0:1, :] * blocks[0]
        for f in range(1, freqs):
            total = total + spread_ref[k, f : f + 1, :] * blocks[f]
        flipped = total.T
        turned.append(
            jnp.concatenate([flipped[q * cycles : (q + 1) * cycles] for q in range(4)], axis=1)
        )
    high, low = split(jnp.concatenate(turned, axis=0))
    out = (
        jnp.dot(high, azimuth_ref[0], preferred_element_type=f32)
        + jnp.dot(high, azimuth_ref[1], preferred_element_type=f32)
        + jnp.dot(low, azimuth_ref[0], preferred_element_type=f32)
    )
    for k in range(moments):
        out_ref[k] = out[k * cycles : (k + 1) * cycles]


def params(mib):
    return pltpu.CompilerParams(vmem_limit_bytes=mib << 20)


def local(visibility, beam_blocks, legendre, m_table, mode_counts, moment_weights):
    time_local, modes = visibility.shape[1], visibility.shape[3]
    places = lax.axis_size("ma")
    freqs = lax.axis_size("freq")
    total_time = time_local * places
    slots_all = m_table.shape[0]
    slots = slots_all // places
    cycles = legendre.shape[2]
    moments = moment_weights.shape[0]
    depth = 2 * time_local

    other = lax.ppermute(visibility, "ma", [(i, i ^ 1) for i in range(places)])
    beam, degrees = beam_blocks.reshape(2 * slots, modes, -1), beam_blocks.shape[4]
    rows = modes // PIECES
    head, own, mode_mask, degree_mask, table, spread, line = pl.pallas_call(
        functools.partial(prepare_kernel, norm=1.0 / math.sqrt(total_time), time_local=time_local),
        out_shape=(
            pltpu.VMEM((HEADS, rows, degrees), bf16),
            pltpu.VMEM((depth, modes), bf16),
            pltpu.VMEM((2 * slots, modes), f32),
            pltpu.VMEM((2 * slots, degrees), f32),
            pltpu.VMEM((4 * slots_all, 2 * depth), bf16),
            pltpu.VMEM((moments, freqs, 128), f32),
            pltpu.VMEM((1, slots_all), i32),
        ),
        in_specs=[ANY] * 6,
        out_specs=(VMEM,) * 7,
        scratch_shapes=[
            pltpu.SMEM(m_table.shape, i32),
            pltpu.SMEM(mode_counts.shape, i32),
            pltpu.SMEM(moment_weights.shape, f32),
            pltpu.VMEM((time_local, 2, modes), bf16),
            pltpu.SemaphoreType.DMA((5,)),
            pltpu.SemaphoreType.DMA((HEADS,)),
        ],
        compiler_params=params(54),
        name="prepare",
    )(m_table, mode_counts, moment_weights, m_table[None, :], visibility[0], beam)
    parts = pl.pallas_call(
        transform_kernel,
        out_shape=jax.ShapeDtypeStruct((2 * slots_all, modes // 2), f32),
        in_specs=[VMEM, VMEM, VMEM],
        out_specs=VMEM,
        compiler_params=params(16),
        name="transform",
    )(table, own, other.reshape(depth, modes))
    parts = lax.all_to_all(
        parts.reshape(places, 2 * slots, modes // 2), "ma", split_axis=0, concat_axis=0
    )
    sums, azimuth = pl.pallas_call(
        contract_kernel,
        out_shape=(
            pltpu.VMEM((freqs * places, 128), f32),
            pltpu.VMEM((2, 2 * slots_all, CIRCLE // freqs), bf16),
        ),
        in_specs=[VMEM, VMEM, VMEM, VMEM, VMEM, ANY, ANY],
        out_specs=(VMEM, VMEM),
        scratch_shapes=[
            pltpu.VMEM((2 * slots, cycles // 128, 128), f32),
            pltpu.VMEM(beam.shape, bf16),
            pltpu.VMEM(legendre.shape, bf16),
            pltpu.SemaphoreType.DMA((3 * slots * PIECES - HEADS,)),
        ],
        compiler_params=params(48),
        name="contract",
    )(parts, mode_mask, degree_mask, line, head, beam, legendre)
    sums = lax.all_to_all(
        sums[:, None, :], ("freq", "ma"), split_axis=0, concat_axis=0
    ).reshape(freqs * places, 128)
    return pl.pallas_call(
        synthesis_kernel,
        out_shape=jax.ShapeDtypeStruct((moments, cycles // places, CIRCLE // freqs), f32),
        in_specs=[VMEM, VMEM, VMEM],
        out_specs=VMEM,
        compiler_params=params(16),
        name="synthesis",
    )(spread, sums, azimuth)


def solution(mesh):
    placed = (
        P("freq", "ma", None, None),
        P("freq", "ma", None, None, None),
        P("ma", None, None),
        P(),
        P(),
        P(),
    )
    return jax.shard_map(
        local, mesh=mesh, in_specs=placed, out_specs=P(None, "ma", "freq"), check_vma=False
    )
```

```python
import functools
import math

import jax
import jax.numpy as jnp
from jax import lax
from jax.experimental import pallas as pl
from jax.experimental.pallas import tpu as pltpu
from jax.sharding import PartitionSpec as P

f32, bf16, i32 = jnp.float32, jnp.bfloat16, jnp.int32
f16 = jnp.float16
LIFT = 32.0
PIECES = 4
HEADS = 4
CIRCLE = 2048
VMEM = pl.BlockSpec(memory_space=pltpu.VMEM)
ANY = pl.BlockSpec(memory_space=pl.ANY)
SMEM = pl.BlockSpec(memory_space=pltpu.SMEM)


def iota(shape, dim):
    return lax.broadcasted_iota(i32, shape, dim)


def cos_of_index(index):
    folded = jnp.abs((index & (CIRCLE - 1)) - CIRCLE // 2) - CIRCLE // 4
    x = folded.astype(f32) * f32(2.0 * math.pi / CIRCLE)
    y = x * x
    poly = f32(1.0 / math.factorial(13))
    for n in (11, 9, 7, 5, 3):
        poly = poly * y + f32((-1.0) ** (n // 2) / math.factorial(n))
    return x + x * y * poly


def select_m(m_ref, slots):
    lanes = iota((slots.shape[0], m_ref.shape[1]), 1)
    return jnp.sum(jnp.where(lanes == slots, m_ref[...], 0).astype(f32), axis=1, keepdims=True).astype(i32)


def split(x):
    high = x.astype(bf16)
    return high, (x - high.astype(f32)).astype(bf16)


def time_table(m_ref, table_ref, time_local):
    place = lax.axis_index("ma")
    rows, columns = table_ref.shape[0] // 2, table_ref.shape[1] // 2
    m_rows = select_m(m_ref, iota((rows, 1), 0) >> 1)
    out_part = iota((rows, columns), 0) & 1
    column = iota((rows, columns), 1)
    quarter = ((column & 1) - out_part) * (CIRCLE // 4)
    for other in range(2):
        first = (place ^ other) * time_local
        values = cos_of_index(m_rows * (first + (column >> 1)) - quarter)
        high, low = split(values)
        where = slice(other * columns, (other + 1) * columns)
        table_ref[:rows, where] = high
        table_ref[rows:, where] = low


def transform_kernel(table_ref, own_ref, other_ref, out_ref):
    half = out_ref.shape[1]
    first = pl.multiple_of((lax.axis_index("ma") & 1) * half, half)
    depth = own_ref.shape[0]
    total = jnp.dot(
        table_ref[:, :depth], own_ref[:, pl.ds(first, half)], preferred_element_type=f32
    ) + jnp.dot(
        table_ref[:, depth:], other_ref[:, pl.ds(first, half)], preferred_element_type=f32
    )
    rows = out_ref.shape[0]
    out_ref[...] = (total[:rows] + total[rows:]) * f32(LIFT)


def prepare_kernel(
    m_hbm, count_hbm, weight_hbm, m_line_hbm, own_hbm, beam_hbm,
    head_ref, own_ref, mode_ref, degree_ref, table_ref, spread_ref, line_ref,
    m_ref, count_ref, weight_ref, own, small_sems, sems, *, norm, time_local
):
    small = [
        pltpu.make_async_copy(source, target, small_sems.at[n])
        for n, (source, target) in enumerate(
            (
                (m_line_hbm, line_ref),
                (own_hbm, own),
                (m_hbm, m_ref),
                (count_hbm, count_ref),
                (weight_hbm, weight_ref),
            )
        )
    ]
    rows = head_ref.shape[1]
    heads = [
        pltpu.make_async_copy(
            beam_hbm.at[j // PIECES, pl.ds(j % PIECES * rows, rows)], head_ref.at[j], sems.at[j]
        )
        for j in range(head_ref.shape[0])
    ]
    for copy in small + heads:
        copy.start()
    small[0].wait()
    time_table(line_ref, table_ref, time_local)
    small[1].wait()
    own_ref[...] = own[...].reshape(own_ref.shape)
    for copy in small[2:]:
        copy.wait()
    place = lax.axis_index("ma")
    slots = mode_ref.shape[0] // 2
    m_own = [m_ref[place * slots + j] for j in range(slots)]
    shape = mode_ref.shape
    counts = jnp.zeros(shape, i32)
    for j in range(slots):
        counts = jnp.where(iota(shape, 0) >> 1 == j, count_ref[m_own[j]], counts)
    mode_ref[...] = jnp.where(iota(shape, 1) < counts, f32(norm), f32(0.0))
    shape = degree_ref.shape
    firsts = jnp.zeros(shape, i32)
    for j in range(slots):
        firsts = jnp.where(iota(shape, 0) >> 1 == j, m_own[j], firsts)
    degree_ref[...] = jnp.where(iota(shape, 1) >= firsts, f32(1.0), f32(0.0))
    for k in range(weight_ref.shape[0]):
        for f in range(weight_ref.shape[1]):
            spread_ref[k, f : f + 1, :] = jnp.full((1, 128), weight_ref[k, f], f32)
    for copy in heads:
        copy.wait()


def azimuth_table(m_ref, table_ref):
    rows, pixels = table_ref.shape[1:]
    row = iota((rows, 1), 0)
    m_rows = select_m(m_ref, 2 * (row & 31) + (row >> 6))
    weights = jnp.where(m_rows == 0, 1.0, 2.0).astype(f32) * f32(1.0 / math.sqrt(rows))
    first = lax.axis_index("freq") * pixels
    index = m_rows * (first + iota((rows, pixels), 1)) + ((row >> 5) & 1) * (CIRCLE // 4)
    table_ref[0], table_ref[1] = split(cos_of_index(index) * weights)


def contract_kernel(
    parts_ref, mode_ref, degree_ref, line_ref, head_ref, beam_hbm, legendre_hbm,
    out_ref, azimuth_ref, sums, beam, legendre, sems
):
    heads, rows = head_ref.shape[:2]
    slots = legendre_hbm.shape[0]
    pieces = [
        (False, 2 * j + d, part) for j in range(slots) for d in range(2) for part in range(PIECES)
    ][heads:]
    for j in range(slots):
        after = [n for n, piece in enumerate(pieces) if not piece[0] and piece[1] < 2 * (j + 1)]
        pieces[after[-1] + 1 : after[-1] + 1] = [(True, j, part) for part in range(PIECES)]
    copies = {}
    for n, piece in enumerate(pieces):
        is_legendre, j, part = piece
        source, target = (legendre_hbm, legendre) if is_legendre else (beam_hbm, beam)
        place = pl.ds(part * rows, rows)
        copies[piece] = pltpu.make_async_copy(source.at[j, place], target.at[j, place], sems.at[n])
        copies[piece].start()
    azimuth_table(line_ref, azimuth_ref)

    def product(left, is_legendre, j):
        total = None
        for part in range(PIECES):
            place = slice(part * rows, (part + 1) * rows)
            piece = (is_legendre, j, part)
            if piece in copies:
                copies[piece].wait()
                block = (legendre if is_legendre else beam)[j, place, :]
            else:
                block = head_ref[j * PIECES + part]
            term = jnp.dot(left[:, place], block, preferred_element_type=f32)
            total = term if total is None else total + term
        return total

    halves = []
    for core in range(2):
        total = parts_ref[core]
        for source in range(core + 2, parts_ref.shape[0], 2):
            total = total + parts_ref[source]
        halves.append(total)
    spectra = (jnp.concatenate(halves, axis=1) * mode_ref[...]).astype(bf16)
    cycles = legendre.shape[2]
    for j in range(slots):
        with_real = product(spectra, False, 2 * j)
        with_imag = product(spectra, False, 2 * j + 1)
        re, im = 2 * j, 2 * j + 1
        coeffs = jnp.concatenate(
            [
                with_real[re : re + 1] + with_imag[im : im + 1],
                with_real[im : im + 1] - with_imag[re : re + 1],
            ],
            axis=0,
        )
        cycle = product((coeffs * degree_ref[re : re + 2, :]).astype(bf16), True, j)
        for c in range(2):
            for g in range(cycles // 128):
                sums[2 * j + c, pl.ds(g, 1), :] = cycle[c : c + 1, g * 128 : (g + 1) * 128]
    block = iota((cycles // 128, 128), 1) >> 5
    copies = out_ref.shape[0] // (cycles // 32)
    for a in range(4):
        value = sums[0] if a == 0 else pltpu.roll(sums[0], 128 - 32 * a, 1)
        for q in range(1, 4):
            moved = sums[q] if a == q else pltpu.roll(sums[q], (32 * (q - a)) % 128, 1)
            value = jnp.where(block == q, moved, value)
        for f in range(copies):
            out_ref[pl.ds(f * (cycles // 32) + a, cycles // 128, stride=4), :] = value


def synthesis_kernel(spread_ref, sums_ref, azimuth_ref, out_ref):
    moments, cycles, _ = out_ref.shape
    freqs = spread_ref.shape[1]
    owners = sums_ref.shape[0] // freqs
    blocks = [sums_ref[f * owners : (f + 1) * owners, :] for f in range(freqs)]
    turned = []
    for k in range(moments):
        total = spread_ref[k, 0:1, :] * blocks[0]
        for f in range(1, freqs):
            total = total + spread_ref[k, f : f + 1, :] * blocks[f]
        flipped = total.T
        turned.append(
            jnp.concatenate([flipped[q * cycles : (q + 1) * cycles] for q in range(4)], axis=1)
        )
    high, low = split(jnp.concatenate(turned, axis=0))
    out = (
        jnp.dot(high, azimuth_ref[0], preferred_element_type=f32)
        + jnp.dot(high, azimuth_ref[1], preferred_element_type=f32)
        + jnp.dot(low, azimuth_ref[0], preferred_element_type=f32)
    )
    for k in range(moments):
        out_ref[k] = out[k * cycles : (k + 1) * cycles]


def params(mib):
    return pltpu.CompilerParams(vmem_limit_bytes=mib << 20)


def local(visibility, beam_blocks, legendre, m_table, mode_counts, moment_weights):
    time_local, modes = visibility.shape[1], visibility.shape[3]
    places = lax.axis_size("ma")
    freqs = lax.axis_size("freq")
    total_time = time_local * places
    slots_all = m_table.shape[0]
    slots = slots_all // places
    cycles = legendre.shape[2]
    moments = moment_weights.shape[0]
    depth = 2 * time_local

    other = lax.ppermute(visibility, "ma", [(i, i ^ 1) for i in range(places)])
    beam, degrees = beam_blocks.reshape(2 * slots, modes, -1), beam_blocks.shape[4]
    rows = modes // PIECES
    head, own, mode_mask, degree_mask, table, spread, line = pl.pallas_call(
        functools.partial(prepare_kernel, norm=1.0 / (LIFT * math.sqrt(total_time)), time_local=time_local),
        out_shape=(
            pltpu.VMEM((HEADS, rows, degrees), bf16),
            pltpu.VMEM((depth, modes), bf16),
            pltpu.VMEM((2 * slots, modes), f32),
            pltpu.VMEM((2 * slots, degrees), f32),
            pltpu.VMEM((4 * slots_all, 2 * depth), bf16),
            pltpu.VMEM((moments, freqs, 128), f32),
            pltpu.VMEM((1, slots_all), i32),
        ),
        in_specs=[ANY] * 6,
        out_specs=(VMEM,) * 7,
        scratch_shapes=[
            pltpu.SMEM(m_table.shape, i32),
            pltpu.SMEM(mode_counts.shape, i32),
            pltpu.SMEM(moment_weights.shape, f32),
            pltpu.VMEM((time_local, 2, modes), bf16),
            pltpu.SemaphoreType.DMA((5,)),
            pltpu.SemaphoreType.DMA((HEADS,)),
        ],
        compiler_params=params(54),
        name="prepare",
    )(m_table, mode_counts, moment_weights, m_table[None, :], visibility[0], beam)
    parts = pl.pallas_call(
        transform_kernel,
        out_shape=jax.ShapeDtypeStruct((2 * slots_all, modes // 2), f32),
        in_specs=[VMEM, VMEM, VMEM],
        out_specs=VMEM,
        compiler_params=params(16),
        name="transform",
    )(table, own, other.reshape(depth, modes))
    parts = lax.all_to_all(
        parts.reshape(places, 2 * slots, modes // 2).astype(f16), "ma", split_axis=0, concat_axis=0
    ).astype(f32)
    sums, azimuth = pl.pallas_call(
        contract_kernel,
        out_shape=(
            pltpu.VMEM((freqs * places, 128), f32),
            pltpu.VMEM((2, 2 * slots_all, CIRCLE // freqs), bf16),
        ),
        in_specs=[VMEM, VMEM, VMEM, VMEM, VMEM, ANY, ANY],
        out_specs=(VMEM, VMEM),
        scratch_shapes=[
            pltpu.VMEM((2 * slots, cycles // 128, 128), f32),
            pltpu.VMEM(beam.shape, bf16),
            pltpu.VMEM(legendre.shape, bf16),
            pltpu.SemaphoreType.DMA((3 * slots * PIECES - HEADS,)),
        ],
        compiler_params=params(48),
        name="contract",
    )(parts, mode_mask, degree_mask, line, head, beam, legendre)
    sums = lax.all_to_all(
        sums[:, None, :], ("freq", "ma"), split_axis=0, concat_axis=0
    ).reshape(freqs * places, 128)
    return pl.pallas_call(
        synthesis_kernel,
        out_shape=jax.ShapeDtypeStruct((moments, cycles // places, CIRCLE // freqs), f32),
        in_specs=[VMEM, VMEM, VMEM],
        out_specs=VMEM,
        compiler_params=params(16),
        name="synthesis",
    )(spread, sums, azimuth)


def solution(mesh):
    placed = (
        P("freq", "ma", None, None),
        P("freq", "ma", None, None, None),
        P("ma", None, None),
        P(),
        P(),
        P(),
    )
    return jax.shard_map(
        local, mesh=mesh, in_specs=placed, out_specs=P(None, "ma", "freq"), check_vma=False
    )
```

```python
import functools
import math

import jax
import jax.numpy as jnp
from jax import lax
from jax.experimental import pallas as pl
from jax.experimental.pallas import tpu as pltpu
from jax.sharding import PartitionSpec as P

f32, bf16, i32 = jnp.float32, jnp.bfloat16, jnp.int32
f16 = jnp.float16
LIFT = 32.0
PIECES = 4
HEADS = 4
CIRCLE = 2048
VMEM = pl.BlockSpec(memory_space=pltpu.VMEM)
ANY = pl.BlockSpec(memory_space=pl.ANY)
SMEM = pl.BlockSpec(memory_space=pltpu.SMEM)


def iota(shape, dim):
    return lax.broadcasted_iota(i32, shape, dim)


def cos_of_index(index):
    folded = jnp.abs((index & (CIRCLE - 1)) - CIRCLE // 2) - CIRCLE // 4
    x = folded.astype(f32) * f32(2.0 * math.pi / CIRCLE)
    y = x * x
    poly = f32(1.0 / math.factorial(13))
    for n in (11, 9, 7, 5, 3):
        poly = poly * y + f32((-1.0) ** (n // 2) / math.factorial(n))
    return x + x * y * poly


def select_m(m_ref, slots):
    lanes = iota((slots.shape[0], m_ref.shape[1]), 1)
    return jnp.sum(jnp.where(lanes == slots, m_ref[...], 0).astype(f32), axis=1, keepdims=True).astype(i32)


def split(x):
    high = x.astype(bf16)
    return high, (x - high.astype(f32)).astype(bf16)


def time_table(m_ref, table_ref, time_local):
    place = lax.axis_index("ma")
    rows, columns = table_ref.shape[0] // 2, table_ref.shape[1] // 2
    m_rows = select_m(m_ref, iota((rows, 1), 0) >> 1)
    out_part = iota((rows, columns), 0) & 1
    column = iota((rows, columns), 1)
    quarter = ((column & 1) - out_part) * (CIRCLE // 4)
    for other in range(2):
        first = (place ^ other) * time_local
        values = cos_of_index(m_rows * (first + (column >> 1)) - quarter)
        high, low = split(values)
        where = slice(other * columns, (other + 1) * columns)
        table_ref[:rows, where] = high
        table_ref[rows:, where] = low


def transform_kernel(table_ref, own_ref, other_ref, out_ref):
    rows, half = out_ref.shape
    place = pl.ds(pl.multiple_of((lax.axis_index("ma") & 1) * half, half), half)
    other = other_ref[:, :, place].reshape(own_ref.shape[0], half)
    both = jnp.concatenate([own_ref[:, place], other], axis=0)
    total = jnp.dot(table_ref[...], both, preferred_element_type=f32)
    out_ref[...] = (total[:rows] + total[rows:]) * f32(LIFT)


def prepare_kernel(
    m_hbm, count_hbm, weight_hbm, m_line_hbm, own_hbm, beam_hbm,
    head_ref, own_ref, mode_ref, degree_ref, table_ref, spread_ref, line_ref,
    m_ref, count_ref, weight_ref, own, small_sems, sems, *, norm, time_local
):
    small = [
        pltpu.make_async_copy(source, target, small_sems.at[n])
        for n, (source, target) in enumerate(
            (
                (m_line_hbm, line_ref),
                (own_hbm, own),
                (m_hbm, m_ref),
                (count_hbm, count_ref),
                (weight_hbm, weight_ref),
            )
        )
    ]
    rows = head_ref.shape[1]
    heads = [
        pltpu.make_async_copy(
            beam_hbm.at[j // PIECES, pl.ds(j % PIECES * rows, rows)], head_ref.at[j], sems.at[j]
        )
        for j in range(head_ref.shape[0])
    ]
    for copy in small + heads:
        copy.start()
    small[0].wait()
    time_table(line_ref, table_ref, time_local)
    small[1].wait()
    own_ref[...] = own[...].reshape(own_ref.shape)
    for copy in small[2:]:
        copy.wait()
    place = lax.axis_index("ma")
    slots = mode_ref.shape[0] // 2
    m_own = [m_ref[place * slots + j] for j in range(slots)]
    shape = mode_ref.shape
    counts = jnp.zeros(shape, i32)
    for j in range(slots):
        counts = jnp.where(iota(shape, 0) >> 1 == j, count_ref[m_own[j]], counts)
    mode_ref[...] = jnp.where(iota(shape, 1) < counts, f32(norm), f32(0.0))
    shape = degree_ref.shape
    firsts = jnp.zeros(shape, i32)
    for j in range(slots):
        firsts = jnp.where(iota(shape, 0) >> 1 == j, m_own[j], firsts)
    degree_ref[...] = jnp.where(iota(shape, 1) >= firsts, f32(1.0), f32(0.0))
    for k in range(weight_ref.shape[0]):
        for f in range(weight_ref.shape[1]):
            spread_ref[k, f : f + 1, :] = jnp.full((1, 128), weight_ref[k, f], f32)
    for copy in heads:
        copy.wait()


def azimuth_table(m_ref, table_ref):
    rows, pixels = table_ref.shape[1:]
    row = iota((rows, 1), 0)
    m_rows = select_m(m_ref, 2 * (row & 31) + (row >> 6))
    weights = jnp.where(m_rows == 0, 1.0, 2.0).astype(f32) * f32(1.0 / math.sqrt(rows))
    first = lax.axis_index("freq") * pixels
    index = m_rows * (first + iota((rows, pixels), 1)) + ((row >> 5) & 1) * (CIRCLE // 4)
    table_ref[0], table_ref[1] = split(cos_of_index(index) * weights)


def contract_kernel(
    parts_ref, mode_ref, degree_ref, line_ref, head_ref, beam_hbm, legendre_hbm,
    out_ref, azimuth_ref, sums, beam, legendre, sems
):
    heads, rows = head_ref.shape[:2]
    slots = legendre_hbm.shape[0]
    pieces = [
        (False, 2 * j + d, part) for j in range(slots) for d in range(2) for part in range(PIECES)
    ][heads:]
    for j in range(slots):
        after = [n for n, piece in enumerate(pieces) if not piece[0] and piece[1] < 2 * (j + 1)]
        pieces[after[-1] + 1 : after[-1] + 1] = [(True, j, part) for part in range(PIECES)]
    copies = {}
    for n, piece in enumerate(pieces):
        is_legendre, j, part = piece
        source, target = (legendre_hbm, legendre) if is_legendre else (beam_hbm, beam)
        place = pl.ds(part * rows, rows)
        copies[piece] = pltpu.make_async_copy(source.at[j, place], target.at[j, place], sems.at[n])
        copies[piece].start()
    azimuth_table(line_ref, azimuth_ref)

    def product(left, is_legendre, j):
        total = None
        for part in range(PIECES):
            place = slice(part * rows, (part + 1) * rows)
            piece = (is_legendre, j, part)
            if piece in copies:
                copies[piece].wait()
                block = (legendre if is_legendre else beam)[j, place, :]
            else:
                block = head_ref[j * PIECES + part]
            term = jnp.dot(left[:, place], block, preferred_element_type=f32)
            total = term if total is None else total + term
        return total

    halves = []
    for core in range(2):
        total = parts_ref[core]
        for source in range(core + 2, parts_ref.shape[0], 2):
            total = total + parts_ref[source]
        halves.append(total)
    spectra = (jnp.concatenate(halves, axis=1) * mode_ref[...]).astype(bf16)
    cycles = legendre.shape[2]
    for j in range(slots):
        with_real = product(spectra, False, 2 * j)
        with_imag = product(spectra, False, 2 * j + 1)
        re, im = 2 * j, 2 * j + 1
        coeffs = jnp.concatenate(
            [
                with_real[re : re + 1] + with_imag[im : im + 1],
                with_real[im : im + 1] - with_imag[re : re + 1],
            ],
            axis=0,
        )
        cycle = product((coeffs * degree_ref[re : re + 2, :]).astype(bf16), True, j)
        for c in range(2):
            for g in range(cycles // 128):
                sums[2 * j + c, pl.ds(g, 1), :] = cycle[c : c + 1, g * 128 : (g + 1) * 128]
    block = iota((cycles // 128, 128), 1) >> 5
    copies = out_ref.shape[0] // (cycles // 32)
    for a in range(4):
        value = sums[0] if a == 0 else pltpu.roll(sums[0], 128 - 32 * a, 1)
        for q in range(1, 4):
            moved = sums[q] if a == q else pltpu.roll(sums[q], (32 * (q - a)) % 128, 1)
            value = jnp.where(block == q, moved, value)
        for f in range(copies):
            out_ref[pl.ds(f * (cycles // 32) + a, cycles // 128, stride=4), :] = value


def synthesis_kernel(spread_ref, sums_ref, azimuth_ref, out_ref):
    moments, cycles, _ = out_ref.shape
    freqs = spread_ref.shape[1]
    owners = sums_ref.shape[0] // freqs
    blocks = [sums_ref[f * owners : (f + 1) * owners, :] for f in range(freqs)]
    turned = []
    for k in range(moments):
        total = spread_ref[k, 0:1, :] * blocks[0]
        for f in range(1, freqs):
            total = total + spread_ref[k, f : f + 1, :] * blocks[f]
        flipped = total.T
        turned.append(
            jnp.concatenate([flipped[q * cycles : (q + 1) * cycles] for q in range(4)], axis=1)
        )
    high, low = split(jnp.concatenate(turned, axis=0))
    out = (
        jnp.dot(high, azimuth_ref[0], preferred_element_type=f32)
        + jnp.dot(high, azimuth_ref[1], preferred_element_type=f32)
        + jnp.dot(low, azimuth_ref[0], preferred_element_type=f32)
    )
    for k in range(moments):
        out_ref[k] = out[k * cycles : (k + 1) * cycles]


def params(mib):
    return pltpu.CompilerParams(vmem_limit_bytes=mib << 20)


def local(visibility, beam_blocks, legendre, m_table, mode_counts, moment_weights):
    time_local, modes = visibility.shape[1], visibility.shape[3]
    places = lax.axis_size("ma")
    freqs = lax.axis_size("freq")
    total_time = time_local * places
    slots_all = m_table.shape[0]
    slots = slots_all // places
    cycles = legendre.shape[2]
    moments = moment_weights.shape[0]
    depth = 2 * time_local

    other = lax.ppermute(visibility, "ma", [(i, i ^ 1) for i in range(places)])
    beam, degrees = beam_blocks.reshape(2 * slots, modes, -1), beam_blocks.shape[4]
    rows = modes // PIECES
    head, own, mode_mask, degree_mask, table, spread, line = pl.pallas_call(
        functools.partial(prepare_kernel, norm=1.0 / (LIFT * math.sqrt(total_time)), time_local=time_local),
        out_shape=(
            pltpu.VMEM((HEADS, rows, degrees), bf16),
            pltpu.VMEM((depth, modes), bf16),
            pltpu.VMEM((2 * slots, modes), f32),
            pltpu.VMEM((2 * slots, degrees), f32),
            pltpu.VMEM((4 * slots_all, 2 * depth), bf16),
            pltpu.VMEM((moments, freqs, 128), f32),
            pltpu.VMEM((1, slots_all), i32),
        ),
        in_specs=[ANY] * 6,
        out_specs=(VMEM,) * 7,
        scratch_shapes=[
            pltpu.SMEM(m_table.shape, i32),
            pltpu.SMEM(mode_counts.shape, i32),
            pltpu.SMEM(moment_weights.shape, f32),
            pltpu.VMEM((time_local, 2, modes), bf16),
            pltpu.SemaphoreType.DMA((5,)),
            pltpu.SemaphoreType.DMA((HEADS,)),
        ],
        compiler_params=params(54),
        name="prepare",
    )(m_table, mode_counts, moment_weights, m_table[None, :], visibility[0], beam)
    parts = pl.pallas_call(
        transform_kernel,
        out_shape=jax.ShapeDtypeStruct((2 * slots_all, modes // 2), f32),
        in_specs=[VMEM, VMEM, VMEM],
        out_specs=VMEM,
        compiler_params=params(16),
        name="transform",
    )(table, own, other[0])
    parts = lax.all_to_all(
        parts.reshape(places, 2 * slots, modes // 2).astype(f16), "ma", split_axis=0, concat_axis=0
    ).astype(f32)
    sums, azimuth = pl.pallas_call(
        contract_kernel,
        out_shape=(
            pltpu.VMEM((freqs * places, 128), f32),
            pltpu.VMEM((2, 2 * slots_all, CIRCLE // freqs), bf16),
        ),
        in_specs=[VMEM, VMEM, VMEM, VMEM, VMEM, ANY, ANY],
        out_specs=(VMEM, VMEM),
        scratch_shapes=[
            pltpu.VMEM((2 * slots, cycles // 128, 128), f32),
            pltpu.VMEM(beam.shape, bf16),
            pltpu.VMEM(legendre.shape, bf16),
            pltpu.SemaphoreType.DMA((3 * slots * PIECES - HEADS,)),
        ],
        compiler_params=params(48),
        name="contract",
    )(parts, mode_mask, degree_mask, line, head, beam, legendre)
    sums = lax.all_to_all(
        sums[:, None, :], ("freq", "ma"), split_axis=0, concat_axis=0
    ).reshape(freqs * places, 128)
    return pl.pallas_call(
        synthesis_kernel,
        out_shape=jax.ShapeDtypeStruct((moments, cycles // places, CIRCLE // freqs), f32),
        in_specs=[VMEM, VMEM, VMEM],
        out_specs=VMEM,
        compiler_params=params(16),
        name="synthesis",
    )(spread, sums, azimuth)


def solution(mesh):
    placed = (
        P("freq", "ma", None, None),
        P("freq", "ma", None, None, None),
        P("ma", None, None),
        P(),
        P(),
        P(),
    )
    return jax.shard_map(
        local, mesh=mesh, in_specs=placed, out_specs=P(None, "ma", "freq"), check_vma=False
    )
```

```python
import functools
import math

import jax
import jax.numpy as jnp
from jax import lax
from jax.experimental import pallas as pl
from jax.experimental.pallas import tpu as pltpu
from jax.sharding import Mesh
from jax.sharding import PartitionSpec as P

f32, bf16, i32 = jnp.float32, jnp.bfloat16, jnp.int32
f16 = jnp.float16
LIFT = 32.0
PIECES = 4
HEADS = 4
SWAP = [(0, 1), (1, 0)]
CIRCLE = 2048
VMEM = pl.BlockSpec(memory_space=pltpu.VMEM)
ANY = pl.BlockSpec(memory_space=pl.ANY)
SMEM = pl.BlockSpec(memory_space=pltpu.SMEM)


def own_place():
    return lax.axis_index("chip") * 2 + lax.axis_index("core")


def iota(shape, dim):
    return lax.broadcasted_iota(i32, shape, dim)


def cos_of_index(index):
    folded = jnp.abs((index & (CIRCLE - 1)) - CIRCLE // 2) - CIRCLE // 4
    x = folded.astype(f32) * f32(2.0 * math.pi / CIRCLE)
    y = x * x
    poly = f32(1.0 / math.factorial(13))
    for n in (11, 9, 7, 5, 3):
        poly = poly * y + f32((-1.0) ** (n // 2) / math.factorial(n))
    return x + x * y * poly


def select_m(m_ref, slots):
    lanes = iota((slots.shape[0], m_ref.shape[1]), 1)
    return jnp.sum(jnp.where(lanes == slots, m_ref[...], 0).astype(f32), axis=1, keepdims=True).astype(i32)


def split(x):
    high = x.astype(bf16)
    return high, (x - high.astype(f32)).astype(bf16)


def time_table(m_ref, table_ref, time_local):
    place = own_place()
    rows, columns = table_ref.shape[0] // 2, table_ref.shape[1] // 2
    m_rows = select_m(m_ref, iota((rows, 1), 0) >> 1)
    out_part = iota((rows, columns), 0) & 1
    column = iota((rows, columns), 1)
    quarter = ((column & 1) - out_part) * (CIRCLE // 4)
    for other in range(2):
        first = (place ^ other) * time_local
        values = cos_of_index(m_rows * (first + (column >> 1)) - quarter)
        high, low = split(values)
        where = slice(other * columns, (other + 1) * columns)
        table_ref[:rows, where] = high
        table_ref[rows:, where] = low


def transform_kernel(table_ref, own_ref, other_ref, out_ref):
    rows, half = out_ref.shape
    place = pl.ds(pl.multiple_of(lax.axis_index("core") * half, half), half)
    other = other_ref[:, :, place].reshape(own_ref.shape[0], half)
    both = jnp.concatenate([own_ref[:, place], other], axis=0)
    total = jnp.dot(table_ref[...], both, preferred_element_type=f32)
    out_ref[...] = (total[:rows] + total[rows:]) * f32(LIFT)


def prepare_kernel(
    m_hbm, count_hbm, weight_hbm, m_line_hbm, own_hbm, beam_hbm,
    head_ref, own_ref, mode_ref, degree_ref, table_ref, spread_ref, line_ref,
    m_ref, count_ref, weight_ref, own, small_sems, sems, *, norm, time_local
):
    small = [
        pltpu.make_async_copy(source, target, small_sems.at[n])
        for n, (source, target) in enumerate(
            (
                (m_line_hbm, line_ref),
                (own_hbm, own),
                (m_hbm, m_ref),
                (count_hbm, count_ref),
                (weight_hbm, weight_ref),
            )
        )
    ]
    rows = head_ref.shape[1]
    heads = [
        pltpu.make_async_copy(
            beam_hbm.at[j // PIECES, pl.ds(j % PIECES * rows, rows)], head_ref.at[j], sems.at[j]
        )
        for j in range(head_ref.shape[0])
    ]
    for copy in small + heads:
        copy.start()
    small[0].wait()
    time_table(line_ref, table_ref, time_local)
    small[1].wait()
    own_ref[...] = own[...].reshape(own_ref.shape)
    for copy in small[2:]:
        copy.wait()
    place = own_place()
    slots = mode_ref.shape[0] // 2
    m_own = [m_ref[place * slots + j] for j in range(slots)]
    shape = mode_ref.shape
    counts = jnp.zeros(shape, i32)
    for j in range(slots):
        counts = jnp.where(iota(shape, 0) >> 1 == j, count_ref[m_own[j]], counts)
    mode_ref[...] = jnp.where(iota(shape, 1) < counts, f32(norm), f32(0.0))
    shape = degree_ref.shape
    firsts = jnp.zeros(shape, i32)
    for j in range(slots):
        firsts = jnp.where(iota(shape, 0) >> 1 == j, m_own[j], firsts)
    degree_ref[...] = jnp.where(iota(shape, 1) >= firsts, f32(1.0), f32(0.0))
    for k in range(weight_ref.shape[0]):
        for f in range(weight_ref.shape[1]):
            spread_ref[k, f : f + 1, :] = jnp.full((1, 128), weight_ref[k, f], f32)
    for copy in heads:
        copy.wait()


def azimuth_table(m_ref, table_ref):
    rows, pixels = table_ref.shape[1:]
    row = iota((rows, 1), 0)
    m_rows = select_m(m_ref, 2 * (row & 31) + (row >> 6))
    weights = jnp.where(m_rows == 0, 1.0, 2.0).astype(f32) * f32(1.0 / math.sqrt(rows))
    first = lax.axis_index("freq") * pixels
    index = m_rows * (first + iota((rows, pixels), 1)) + ((row >> 5) & 1) * (CIRCLE // 4)
    table_ref[0], table_ref[1] = split(cos_of_index(index) * weights)


def contract_kernel(
    parts_ref, mode_ref, degree_ref, line_ref, head_ref, beam_hbm, legendre_hbm,
    out_ref, swap_ref, azimuth_ref, sums, beam, legendre, sems
):
    heads, rows = head_ref.shape[:2]
    slots = legendre_hbm.shape[0]
    pieces = [
        (False, 2 * j + d, part) for j in range(slots) for d in range(2) for part in range(PIECES)
    ][heads:]
    for j in range(slots):
        after = [n for n, piece in enumerate(pieces) if not piece[0] and piece[1] < 2 * (j + 1)]
        pieces[after[-1] + 1 : after[-1] + 1] = [(True, j, part) for part in range(PIECES)]
    copies = {}
    for n, piece in enumerate(pieces):
        is_legendre, j, part = piece
        source, target = (legendre_hbm, legendre) if is_legendre else (beam_hbm, beam)
        place = pl.ds(part * rows, rows)
        copies[piece] = pltpu.make_async_copy(source.at[j, place], target.at[j, place], sems.at[n])
        copies[piece].start()
    azimuth_table(line_ref, azimuth_ref)

    def product(left, is_legendre, j):
        total = None
        for part in range(PIECES):
            place = slice(part * rows, (part + 1) * rows)
            piece = (is_legendre, j, part)
            if piece in copies:
                copies[piece].wait()
                block = (legendre if is_legendre else beam)[j, place, :]
            else:
                block = head_ref[j * PIECES + part]
            term = jnp.dot(left[:, place], block, preferred_element_type=f32)
            total = term if total is None else total + term
        return total

    halves = []
    for core in range(2):
        total = parts_ref[core]
        for source in range(core + 2, parts_ref.shape[0], 2):
            total = total + parts_ref[source]
        halves.append(total)
    spectra = (jnp.concatenate(halves, axis=1) * mode_ref[...]).astype(bf16)
    cycles = legendre.shape[2]
    for j in range(slots):
        with_real = product(spectra, False, 2 * j)
        with_imag = product(spectra, False, 2 * j + 1)
        re, im = 2 * j, 2 * j + 1
        coeffs = jnp.concatenate(
            [
                with_real[re : re + 1] + with_imag[im : im + 1],
                with_real[im : im + 1] - with_imag[re : re + 1],
            ],
            axis=0,
        )
        cycle = product((coeffs * degree_ref[re : re + 2, :]).astype(bf16), True, j)
        for c in range(2):
            for g in range(cycles // 128):
                sums[2 * j + c, pl.ds(g, 1), :] = cycle[c : c + 1, g * 128 : (g + 1) * 128]
    block = iota((cycles // 128, 128), 1) >> 5
    values = []
    for a in range(4):
        value = sums[0] if a == 0 else pltpu.roll(sums[0], 128 - 32 * a, 1)
        for q in range(1, 4):
            moved = sums[q] if a == q else pltpu.roll(sums[q], (32 * (q - a)) % 128, 1)
            value = jnp.where(block == q, moved, value)
        values.append(value)
    core = lax.axis_index("core")
    for half in range(2):
        even, odd = values[2 * half], values[2 * half + 1]
        chips = pl.ds(half, cycles // 128, stride=2)
        out_ref[chips, :] = jnp.where(core == 0, even, odd)
        swap_ref[chips, :] = jnp.where(core == 0, odd, even)


def synthesis_kernel(spread_ref, sums_ref, azimuth_ref, out_ref):
    moments, cycles, _ = out_ref.shape
    freqs = spread_ref.shape[1]
    owners = sums_ref.shape[0] // freqs
    blocks = [sums_ref[f * owners : (f + 1) * owners, :].astype(f32) for f in range(freqs)]
    turned = []
    for k in range(moments):
        total = spread_ref[k, 0:1, :] * blocks[0]
        for f in range(1, freqs):
            total = total + spread_ref[k, f : f + 1, :] * blocks[f]
        flipped = total.T
        turned.append(
            jnp.concatenate([flipped[q * cycles : (q + 1) * cycles] for q in range(4)], axis=1)
        )
    high, low = split(jnp.concatenate(turned, axis=0))
    out = (
        jnp.dot(high, azimuth_ref[0], preferred_element_type=f32)
        + jnp.dot(high, azimuth_ref[1], preferred_element_type=f32)
        + jnp.dot(low, azimuth_ref[0], preferred_element_type=f32)
    )
    for k in range(moments):
        out_ref[k] = out[k * cycles : (k + 1) * cycles]


def params(mib):
    return pltpu.CompilerParams(vmem_limit_bytes=mib << 20)


def local(visibility, beam_blocks, legendre, m_table, mode_counts, moment_weights):
    time_local, modes = visibility.shape[1], visibility.shape[3]
    places = lax.axis_size("chip") * lax.axis_size("core")
    freqs = lax.axis_size("freq")
    total_time = time_local * places
    slots_all = m_table.shape[0]
    slots = slots_all // places
    cycles = legendre.shape[2]
    moments = moment_weights.shape[0]
    depth = 2 * time_local

    other = lax.ppermute(visibility, "core", SWAP)
    beam, degrees = beam_blocks.reshape(2 * slots, modes, -1), beam_blocks.shape[4]
    rows = modes // PIECES
    head, own, mode_mask, degree_mask, table, spread, line = pl.pallas_call(
        functools.partial(prepare_kernel, norm=1.0 / (LIFT * math.sqrt(total_time)), time_local=time_local),
        out_shape=(
            pltpu.VMEM((HEADS, rows, degrees), bf16),
            pltpu.VMEM((depth, modes), bf16),
            pltpu.VMEM((2 * slots, modes), f32),
            pltpu.VMEM((2 * slots, degrees), f32),
            pltpu.VMEM((4 * slots_all, 2 * depth), bf16),
            pltpu.VMEM((moments, freqs, 128), f32),
            pltpu.VMEM((1, slots_all), i32),
        ),
        in_specs=[ANY] * 6,
        out_specs=(VMEM,) * 7,
        scratch_shapes=[
            pltpu.SMEM(m_table.shape, i32),
            pltpu.SMEM(mode_counts.shape, i32),
            pltpu.SMEM(moment_weights.shape, f32),
            pltpu.VMEM((time_local, 2, modes), bf16),
            pltpu.SemaphoreType.DMA((5,)),
            pltpu.SemaphoreType.DMA((HEADS,)),
        ],
        compiler_params=params(54),
        name="prepare",
    )(m_table, mode_counts, moment_weights, m_table[None, :], visibility[0], beam)
    parts = pl.pallas_call(
        transform_kernel,
        out_shape=jax.ShapeDtypeStruct((2 * slots_all, modes // 2), f32),
        in_specs=[VMEM, VMEM, VMEM],
        out_specs=VMEM,
        compiler_params=params(16),
        name="transform",
    )(table, own, other[0])
    parts = lax.all_to_all(
        parts.reshape(places, 2 * slots, modes // 2).astype(f16), ("chip", "core"), split_axis=0, concat_axis=0
    ).astype(f32)
    sums, swapped, azimuth = pl.pallas_call(
        contract_kernel,
        out_shape=(
            pltpu.VMEM((places // 2, 128), f32),
            pltpu.VMEM((places // 2, 128), f32),
            pltpu.VMEM((2, 2 * slots_all, CIRCLE // freqs), bf16),
        ),
        in_specs=[VMEM, VMEM, VMEM, VMEM, VMEM, ANY, ANY],
        out_specs=(VMEM, VMEM, VMEM),
        scratch_shapes=[
            pltpu.VMEM((2 * slots, cycles // 128, 128), f32),
            pltpu.VMEM(beam.shape, bf16),
            pltpu.VMEM(legendre.shape, bf16),
            pltpu.SemaphoreType.DMA((3 * slots * PIECES - HEADS,)),
        ],
        compiler_params=params(48),
        name="contract",
    )(parts, mode_mask, degree_mask, line, head, beam, legendre)
    swapped = lax.ppermute(swapped, "core", SWAP)
    first = lax.axis_index("core") == 0
    pair = jnp.stack(
        [jnp.where(first, sums, swapped), jnp.where(first, swapped, sums)], axis=1
    ).astype(bf16)
    sums = lax.all_to_all(
        jnp.broadcast_to(pair[None], (freqs,) + pair.shape).reshape((-1,) + pair.shape[1:]),
        ("freq", "chip"),
        split_axis=0,
        concat_axis=0,
    ).reshape(freqs * places, 128)
    return pl.pallas_call(
        synthesis_kernel,
        out_shape=jax.ShapeDtypeStruct((moments, cycles // places, CIRCLE // freqs), f32),
        in_specs=[VMEM, VMEM, VMEM],
        out_specs=VMEM,
        compiler_params=params(16),
        name="synthesis",
    )(spread, sums, azimuth)


def solution(mesh):
    freqs, places = mesh.devices.shape
    fine = Mesh(mesh.devices.reshape(freqs, places // 2, 2), ("freq", "chip", "core"))
    ma = ("chip", "core")
    placed = (
        P("freq", ma, None, None),
        P("freq", ma, None, None, None),
        P(ma, None, None),
        P(),
        P(),
        P(),
    )
    return jax.shard_map(
        local, mesh=fine, in_specs=placed, out_specs=P(None, ma, "freq"), check_vma=False
    )
```

```python
import functools
import math

import jax
import jax.numpy as jnp
from jax import lax
from jax.experimental import pallas as pl
from jax.experimental.pallas import tpu as pltpu
from jax.sharding import Mesh
from jax.sharding import PartitionSpec as P

f32, bf16, i32 = jnp.float32, jnp.bfloat16, jnp.int32
f16 = jnp.float16
LIFT = 32.0
PIECES = 4
HEADS = 4
SWAP = [(0, 1), (1, 0)]
CIRCLE = 2048
VMEM = pl.BlockSpec(memory_space=pltpu.VMEM)
ANY = pl.BlockSpec(memory_space=pl.ANY)
SMEM = pl.BlockSpec(memory_space=pltpu.SMEM)


def own_place():
    return lax.axis_index("chip") * 2 + lax.axis_index("core")


def iota(shape, dim):
    return lax.broadcasted_iota(i32, shape, dim)


def cos_of_index(index):
    folded = jnp.abs((index & (CIRCLE - 1)) - CIRCLE // 2) - CIRCLE // 4
    x = folded.astype(f32) * f32(2.0 * math.pi / CIRCLE)
    y = x * x
    poly = f32(1.0 / math.factorial(13))
    for n in (11, 9, 7, 5, 3):
        poly = poly * y + f32((-1.0) ** (n // 2) / math.factorial(n))
    return x + x * y * poly


def select_m(m_ref, slots):
    lanes = iota((slots.shape[0], m_ref.shape[1]), 1)
    return jnp.sum(jnp.where(lanes == slots, m_ref[...], 0).astype(f32), axis=1, keepdims=True).astype(i32)


def split(x):
    high = x.astype(bf16)
    return high, (x - high.astype(f32)).astype(bf16)


def time_table(m_ref, shape, time_local, other):
    m_rows = select_m(m_ref, iota((shape[0], 1), 0) >> 1)
    column = iota(shape, 1)
    quarter = ((column & 1) - (iota(shape, 0) & 1)) * (CIRCLE // 4)
    first = (own_place() ^ other) * time_local
    return jnp.concatenate(split(cos_of_index(m_rows * (first + (column >> 1)) - quarter)), axis=0)


def half_transform(table, block_ref):
    rows, depth = table.shape[0] // 2, table.shape[1]
    half = block_ref.shape[2] // 2
    place = pl.ds(pl.multiple_of(lax.axis_index("core") * half, half), half)
    block = block_ref[:, :, place].reshape(depth, half)
    total = jnp.dot(table, block, preferred_element_type=f32)
    return (total[:rows] + total[rows:]) * f32(LIFT)


def transform_kernel(table_ref, own_ref, other_ref, out_ref):
    out_ref[...] = own_ref[...] + half_transform(table_ref[...], other_ref)


def prepare_kernel(
    m_hbm, count_hbm, weight_hbm, m_line_hbm, own_hbm, beam_hbm,
    head_ref, own_ref, mode_ref, degree_ref, table_ref, spread_ref, line_ref,
    m_ref, count_ref, weight_ref, own, small_sems, sems, *, norm, time_local
):
    small = [
        pltpu.make_async_copy(source, target, small_sems.at[n])
        for n, (source, target) in enumerate(
            (
                (m_line_hbm, line_ref),
                (own_hbm, own),
                (m_hbm, m_ref),
                (count_hbm, count_ref),
                (weight_hbm, weight_ref),
            )
        )
    ]
    rows = head_ref.shape[1]
    heads = [
        pltpu.make_async_copy(
            beam_hbm.at[j // PIECES, pl.ds(j % PIECES * rows, rows)], head_ref.at[j], sems.at[j]
        )
        for j in range(head_ref.shape[0])
    ]
    for copy in small[:1] + heads + small[1:]:
        copy.start()
    small[0].wait()
    shape = table_ref.shape[0] // 2, table_ref.shape[1]
    table_ref[...] = time_table(line_ref, shape, time_local, 1)
    table = time_table(line_ref, shape, time_local, 0)
    small[1].wait()
    own_ref[...] = half_transform(table, own)
    for copy in small[2:]:
        copy.wait()
    place = own_place()
    slots = mode_ref.shape[0] // 2
    m_own = [m_ref[place * slots + j] for j in range(slots)]
    shape = mode_ref.shape
    counts = jnp.zeros(shape, i32)
    for j in range(slots):
        counts = jnp.where(iota(shape, 0) >> 1 == j, count_ref[m_own[j]], counts)
    mode_ref[...] = jnp.where(iota(shape, 1) < counts, f32(norm), f32(0.0))
    shape = degree_ref.shape
    firsts = jnp.zeros(shape, i32)
    for j in range(slots):
        firsts = jnp.where(iota(shape, 0) >> 1 == j, m_own[j], firsts)
    degree_ref[...] = jnp.where(iota(shape, 1) >= firsts, f32(1.0), f32(0.0))
    for k in range(weight_ref.shape[0]):
        for f in range(weight_ref.shape[1]):
            spread_ref[k, f : f + 1, :] = jnp.full((1, 128), weight_ref[k, f], f32)
    for copy in heads:
        copy.wait()


def azimuth_table(m_ref, table_ref):
    rows, pixels = table_ref.shape[1:]
    row = iota((rows, 1), 0)
    m_rows = select_m(m_ref, 2 * (row & 31) + (row >> 6))
    weights = jnp.where(m_rows == 0, 1.0, 2.0).astype(f32) * f32(1.0 / math.sqrt(rows))
    first = lax.axis_index("freq") * pixels
    index = m_rows * (first + iota((rows, pixels), 1)) + ((row >> 5) & 1) * (CIRCLE // 4)
    table_ref[0], table_ref[1] = split(cos_of_index(index) * weights)


def contract_kernel(
    parts_ref, mode_ref, degree_ref, line_ref, head_ref, beam_hbm, legendre_hbm,
    out_ref, swap_ref, azimuth_ref, sums, beam, legendre, sems
):
    heads, rows = head_ref.shape[:2]
    slots = legendre_hbm.shape[0]
    pieces = [
        (False, 2 * j + d, part) for j in range(slots) for d in range(2) for part in range(PIECES)
    ][heads:]
    for j in range(slots):
        after = [n for n, piece in enumerate(pieces) if not piece[0] and piece[1] < 2 * (j + 1)]
        pieces[after[-1] + 1 : after[-1] + 1] = [(True, j, part) for part in range(PIECES)]
    copies = {}
    for n, piece in enumerate(pieces):
        is_legendre, j, part = piece
        source, target = (legendre_hbm, legendre) if is_legendre else (beam_hbm, beam)
        place = pl.ds(part * rows, rows)
        copies[piece] = pltpu.make_async_copy(source.at[j, place], target.at[j, place], sems.at[n])
        copies[piece].start()
    azimuth_table(line_ref, azimuth_ref)

    def product(left, is_legendre, j, total=None):
        for part in range(PIECES):
            place = slice(part * rows, (part + 1) * rows)
            piece = (is_legendre, j, part)
            if piece in copies:
                copies[piece].wait()
                block = (legendre if is_legendre else beam)[j, place, :]
            else:
                block = head_ref[j * PIECES + part]
            term = jnp.dot(left[:, place], block, preferred_element_type=f32)
            total = term if total is None else total + term
        return total

    halves = []
    for core in range(2):
        total = parts_ref[core]
        for source in range(core + 2, parts_ref.shape[0], 2):
            total = total + parts_ref[source]
        halves.append(total)
    spectra = jnp.concatenate(halves, axis=1) * mode_ref[...]
    turned = []
    for j in range(slots):
        turned += [spectra[2 * j + 1 : 2 * j + 2], -spectra[2 * j : 2 * j + 1]]
    turned = jnp.concatenate(turned, axis=0).astype(bf16)
    spectra = spectra.astype(bf16)
    cycles = legendre.shape[2]
    for j in range(slots):
        coeffs = product(spectra, False, 2 * j)
        coeffs = product(turned, False, 2 * j + 1, coeffs)
        cycle = product((coeffs * degree_ref[...]).astype(bf16), True, j)
        for c in range(2):
            for g in range(cycles // 128):
                sums[2 * j + c, pl.ds(g, 1), :] = cycle[2 * j + c : 2 * j + c + 1, g * 128 : (g + 1) * 128]
    block = iota((cycles // 128, 128), 1) >> 5
    values = []
    for a in range(4):
        value = sums[0] if a == 0 else pltpu.roll(sums[0], 128 - 32 * a, 1)
        for q in range(1, 4):
            moved = sums[q] if a == q else pltpu.roll(sums[q], (32 * (q - a)) % 128, 1)
            value = jnp.where(block == q, moved, value)
        values.append(value)
    core = lax.axis_index("core")
    for half in range(2):
        even, odd = values[2 * half], values[2 * half + 1]
        chips = pl.ds(half, cycles // 128, stride=2)
        out_ref[chips, :] = jnp.where(core == 0, even, odd)
        swap_ref[chips, :] = jnp.where(core == 0, odd, even)


def synthesis_kernel(spread_ref, sums_ref, azimuth_ref, out_ref):
    moments, cycles, _ = out_ref.shape
    freqs = spread_ref.shape[1]
    owners = sums_ref.shape[0] // freqs
    blocks = [sums_ref[f * owners : (f + 1) * owners, :].astype(f32) for f in range(freqs)]
    turned = []
    for k in range(moments):
        total = spread_ref[k, 0:1, :] * blocks[0]
        for f in range(1, freqs):
            total = total + spread_ref[k, f : f + 1, :] * blocks[f]
        flipped = total.T
        turned.append(
            jnp.concatenate([flipped[q * cycles : (q + 1) * cycles] for q in range(4)], axis=1)
        )
    high, low = split(jnp.concatenate(turned, axis=0))
    out = (
        jnp.dot(high, azimuth_ref[0], preferred_element_type=f32)
        + jnp.dot(high, azimuth_ref[1], preferred_element_type=f32)
        + jnp.dot(low, azimuth_ref[0], preferred_element_type=f32)
    )
    for k in range(moments):
        out_ref[k] = out[k * cycles : (k + 1) * cycles]


def params(mib):
    return pltpu.CompilerParams(vmem_limit_bytes=mib << 20)


def local(visibility, beam_blocks, legendre, m_table, mode_counts, moment_weights):
    time_local, modes = visibility.shape[1], visibility.shape[3]
    places = lax.axis_size("chip") * lax.axis_size("core")
    freqs = lax.axis_size("freq")
    total_time = time_local * places
    slots_all = m_table.shape[0]
    slots = slots_all // places
    cycles = legendre.shape[2]
    moments = moment_weights.shape[0]
    depth = 2 * time_local

    other = lax.ppermute(visibility, "core", SWAP)
    beam, degrees = beam_blocks.reshape(2 * slots, modes, -1), beam_blocks.shape[4]
    rows = modes // PIECES
    head, own, mode_mask, degree_mask, table, spread, line = pl.pallas_call(
        functools.partial(prepare_kernel, norm=1.0 / (LIFT * math.sqrt(total_time)), time_local=time_local),
        out_shape=(
            pltpu.VMEM((HEADS, rows, degrees), bf16),
            pltpu.VMEM((2 * slots_all, modes // 2), f32),
            pltpu.VMEM((2 * slots, modes), f32),
            pltpu.VMEM((2 * slots, degrees), f32),
            pltpu.VMEM((4 * slots_all, depth), bf16),
            pltpu.VMEM((moments, freqs, 128), f32),
            pltpu.VMEM((1, slots_all), i32),
        ),
        in_specs=[ANY] * 6,
        out_specs=(VMEM,) * 7,
        scratch_shapes=[
            pltpu.SMEM(m_table.shape, i32),
            pltpu.SMEM(mode_counts.shape, i32),
            pltpu.SMEM(moment_weights.shape, f32),
            pltpu.VMEM((time_local, 2, modes), bf16),
            pltpu.SemaphoreType.DMA((5,)),
            pltpu.SemaphoreType.DMA((HEADS,)),
        ],
        compiler_params=params(54),
        name="prepare",
    )(m_table, mode_counts, moment_weights, m_table[None, :], visibility[0], beam)
    parts = pl.pallas_call(
        transform_kernel,
        out_shape=jax.ShapeDtypeStruct((2 * slots_all, modes // 2), f32),
        in_specs=[VMEM, VMEM, VMEM],
        out_specs=VMEM,
        compiler_params=params(16),
        name="transform",
    )(table, own, other[0])
    parts = lax.all_to_all(
        parts.reshape(places, 2 * slots, modes // 2).astype(f16), ("chip", "core"), split_axis=0, concat_axis=0
    ).astype(f32)
    sums, swapped, azimuth = pl.pallas_call(
        contract_kernel,
        out_shape=(
            pltpu.VMEM((places // 2, 128), f32),
            pltpu.VMEM((places // 2, 128), f32),
            pltpu.VMEM((2, 2 * slots_all, CIRCLE // freqs), bf16),
        ),
        in_specs=[VMEM, VMEM, VMEM, VMEM, VMEM, ANY, ANY],
        out_specs=(VMEM, VMEM, VMEM),
        scratch_shapes=[
            pltpu.VMEM((2 * slots, cycles // 128, 128), f32),
            pltpu.VMEM(beam.shape, bf16),
            pltpu.VMEM(legendre.shape, bf16),
            pltpu.SemaphoreType.DMA((3 * slots * PIECES - HEADS,)),
        ],
        compiler_params=params(48),
        name="contract",
    )(parts, mode_mask, degree_mask, line, head, beam, legendre)
    swapped = lax.ppermute(swapped, "core", SWAP)
    first = lax.axis_index("core") == 0
    pair = jnp.stack(
        [jnp.where(first, sums, swapped), jnp.where(first, swapped, sums)], axis=1
    ).astype(bf16)
    sums = lax.all_to_all(
        jnp.broadcast_to(pair[None], (freqs,) + pair.shape).reshape((-1,) + pair.shape[1:]),
        ("freq", "chip"),
        split_axis=0,
        concat_axis=0,
    ).reshape(freqs * places, 128)
    return pl.pallas_call(
        synthesis_kernel,
        out_shape=jax.ShapeDtypeStruct((moments, cycles // places, CIRCLE // freqs), f32),
        in_specs=[VMEM, VMEM, VMEM],
        out_specs=VMEM,
        compiler_params=params(16),
        name="synthesis",
    )(spread, sums, azimuth)


def solution(mesh):
    freqs, places = mesh.devices.shape
    fine = Mesh(mesh.devices.reshape(freqs, places // 2, 2), ("freq", "chip", "core"))
    ma = ("chip", "core")
    placed = (
        P("freq", ma, None, None),
        P("freq", ma, None, None, None),
        P(ma, None, None),
        P(),
        P(),
        P(),
    )
    return jax.shard_map(
        local, mesh=fine, in_specs=placed, out_specs=P(None, ma, "freq"), check_vma=False
    )
```

```python
import functools
import math

import jax
import jax.numpy as jnp
from jax import lax
from jax.experimental import pallas as pl
from jax.experimental.pallas import tpu as pltpu
from jax.sharding import Mesh
from jax.sharding import PartitionSpec as P

f32, bf16, i32 = jnp.float32, jnp.bfloat16, jnp.int32
f16 = jnp.float16
LIFT = 32.0
PIECES = 4
HEADS = 5
SWAP = [(0, 1), (1, 0)]
CIRCLE = 2048
VMEM = pl.BlockSpec(memory_space=pltpu.VMEM)
ANY = pl.BlockSpec(memory_space=pl.ANY)
SMEM = pl.BlockSpec(memory_space=pltpu.SMEM)


def own_place():
    return lax.axis_index("chip") * 2 + lax.axis_index("core")


def iota(shape, dim):
    return lax.broadcasted_iota(i32, shape, dim)


def cos_of_index(index):
    folded = jnp.abs((index & (CIRCLE - 1)) - CIRCLE // 2) - CIRCLE // 4
    x = folded.astype(f32) * f32(2.0 * math.pi / CIRCLE)
    y = x * x
    poly = f32(1.0 / math.factorial(13))
    for n in (11, 9, 7, 5, 3):
        poly = poly * y + f32((-1.0) ** (n // 2) / math.factorial(n))
    return x + x * y * poly


def select_m(m_ref, slots):
    lanes = iota((slots.shape[0], m_ref.shape[1]), 1)
    return jnp.sum(jnp.where(lanes == slots, m_ref[...], 0).astype(f32), axis=1, keepdims=True).astype(i32)


def split(x):
    high = x.astype(bf16)
    return high, (x - high.astype(f32)).astype(bf16)


def time_table(m_ref, table_ref, time_local):
    place = own_place()
    rows, columns = table_ref.shape[0] // 2, table_ref.shape[1] // 2
    m_rows = select_m(m_ref, iota((rows, 1), 0) >> 1)
    out_part = iota((rows, columns), 0) & 1
    column = iota((rows, columns), 1)
    quarter = ((column & 1) - out_part) * (CIRCLE // 4)
    for other in range(2):
        first = (place ^ other) * time_local
        values = cos_of_index(m_rows * (first + (column >> 1)) - quarter)
        high, low = split(values)
        where = slice(other * columns, (other + 1) * columns)
        table_ref[:rows, where] = high
        table_ref[rows:, where] = low


def transform_kernel(table_ref, own_ref, other_ref, out_ref):
    rows, half = out_ref.shape
    place = pl.ds(pl.multiple_of(lax.axis_index("core") * half, half), half)
    other = other_ref[:, :, place].reshape(own_ref.shape[0], half)
    both = jnp.concatenate([own_ref[:, place], other], axis=0)
    total = jnp.dot(table_ref[...], both, preferred_element_type=f32)
    out_ref[...] = (total[:rows] + total[rows:]) * f32(LIFT)


def prepare_kernel(
    m_hbm, count_hbm, weight_hbm, m_line_hbm, own_hbm, beam_hbm,
    head_ref, own_ref, mode_ref, degree_ref, table_ref, spread_ref, line_ref,
    m_ref, count_ref, weight_ref, own, small_sems, sems, *, norm, time_local
):
    small = [
        pltpu.make_async_copy(source, target, small_sems.at[n])
        for n, (source, target) in enumerate(
            (
                (m_line_hbm, line_ref),
                (own_hbm, own),
                (m_hbm, m_ref),
                (count_hbm, count_ref),
                (weight_hbm, weight_ref),
            )
        )
    ]
    rows = head_ref.shape[1]
    heads = [
        pltpu.make_async_copy(
            beam_hbm.at[j // PIECES, pl.ds(j % PIECES * rows, rows)], head_ref.at[j], sems.at[j]
        )
        for j in range(head_ref.shape[0])
    ]
    for copy in small[:1] + heads + small[1:]:
        copy.start()
    small[0].wait()
    time_table(line_ref, table_ref, time_local)
    small[1].wait()
    own_ref[...] = own[...].reshape(own_ref.shape)
    for copy in small[2:]:
        copy.wait()
    place = own_place()
    slots = mode_ref.shape[0] // 2
    m_own = [m_ref[place * slots + j] for j in range(slots)]
    shape = mode_ref.shape
    counts = jnp.zeros(shape, i32)
    for j in range(slots):
        counts = jnp.where(iota(shape, 0) >> 1 == j, count_ref[m_own[j]], counts)
    mode_ref[...] = jnp.where(iota(shape, 1) < counts, f32(norm), f32(0.0))
    shape = degree_ref.shape
    firsts = jnp.zeros(shape, i32)
    for j in range(slots):
        firsts = jnp.where(iota(shape, 0) >> 1 == j, m_own[j], firsts)
    degree_ref[...] = jnp.where(iota(shape, 1) >= firsts, f32(1.0), f32(0.0))
    for k in range(weight_ref.shape[0]):
        for f in range(weight_ref.shape[1]):
            spread_ref[k, f : f + 1, :] = jnp.full((1, 128), weight_ref[k, f], f32)
    for copy in heads:
        copy.wait()


def azimuth_table(m_ref, table_ref):
    rows, pixels = table_ref.shape[1:]
    row = iota((rows, 1), 0)
    m_rows = select_m(m_ref, 2 * (row & 31) + (row >> 6))
    weights = jnp.where(m_rows == 0, 1.0, 2.0).astype(f32) * f32(1.0 / math.sqrt(rows))
    first = lax.axis_index("freq") * pixels
    index = m_rows * (first + iota((rows, pixels), 1)) + ((row >> 5) & 1) * (CIRCLE // 4)
    table_ref[0], table_ref[1] = split(cos_of_index(index) * weights)


def contract_kernel(
    parts_ref, mode_ref, degree_ref, line_ref, head_ref, beam_hbm, legendre_hbm,
    out_ref, swap_ref, azimuth_ref, sums, beam, legendre, sems
):
    heads, rows = head_ref.shape[:2]
    slots = legendre_hbm.shape[0]
    pieces = [
        (False, 2 * j + d, part) for j in range(slots) for d in range(2) for part in range(PIECES)
    ][heads:]
    for j in range(slots):
        after = [n for n, piece in enumerate(pieces) if not piece[0] and piece[1] < 2 * (j + 1)]
        pieces[after[-1] + 1 : after[-1] + 1] = [(True, j, part) for part in range(PIECES)]
    copies = {}
    for n, piece in enumerate(pieces):
        is_legendre, j, part = piece
        source, target = (legendre_hbm, legendre) if is_legendre else (beam_hbm, beam)
        place = pl.ds(part * rows, rows)
        copies[piece] = pltpu.make_async_copy(source.at[j, place], target.at[j, place], sems.at[n])
        copies[piece].start()
    azimuth_table(line_ref, azimuth_ref)

    def product(left, is_legendre, j, total=None):
        for part in range(PIECES):
            place = slice(part * rows, (part + 1) * rows)
            piece = (is_legendre, j, part)
            if piece in copies:
                copies[piece].wait()
                block = (legendre if is_legendre else beam)[j, place, :]
            else:
                block = head_ref[j * PIECES + part]
            term = jnp.dot(left[:, place], block, preferred_element_type=f32)
            total = term if total is None else total + term
        return total

    halves = []
    for core in range(2):
        total = parts_ref[core]
        for source in range(core + 2, parts_ref.shape[0], 2):
            total = total + parts_ref[source]
        halves.append(total)
    spectra = jnp.concatenate(halves, axis=1) * mode_ref[...]
    turned = []
    for j in range(slots):
        turned += [spectra[2 * j + 1 : 2 * j + 2], -spectra[2 * j : 2 * j + 1]]
    turned = jnp.concatenate(turned, axis=0).astype(bf16)
    spectra = spectra.astype(bf16)
    cycles = legendre.shape[2]
    for j in range(slots):
        coeffs = product(spectra, False, 2 * j)
        coeffs = product(turned, False, 2 * j + 1, coeffs)
        cycle = product((coeffs * degree_ref[...]).astype(bf16), True, j)
        for c in range(2):
            for g in range(cycles // 128):
                sums[2 * j + c, pl.ds(g, 1), :] = cycle[2 * j + c : 2 * j + c + 1, g * 128 : (g + 1) * 128]
    block = iota((cycles // 128, 128), 1) >> 5
    values = []
    for a in range(4):
        value = sums[0] if a == 0 else pltpu.roll(sums[0], 128 - 32 * a, 1)
        for q in range(1, 4):
            moved = sums[q] if a == q else pltpu.roll(sums[q], (32 * (q - a)) % 128, 1)
            value = jnp.where(block == q, moved, value)
        values.append(value)
    core = lax.axis_index("core")
    for half in range(2):
        even, odd = values[2 * half], values[2 * half + 1]
        chips = pl.ds(half, cycles // 128, stride=2)
        out_ref[chips, :] = jnp.where(core == 0, even, odd)
        swap_ref[chips, :] = jnp.where(core == 0, odd, even)


def synthesis_kernel(spread_ref, sums_ref, azimuth_ref, out_ref):
    moments, cycles, _ = out_ref.shape
    freqs = spread_ref.shape[1]
    owners = sums_ref.shape[0] // freqs
    blocks = [sums_ref[f * owners : (f + 1) * owners, :].astype(f32) for f in range(freqs)]
    turned = []
    for k in range(moments):
        total = spread_ref[k, 0:1, :] * blocks[0]
        for f in range(1, freqs):
            total = total + spread_ref[k, f : f + 1, :] * blocks[f]
        flipped = total.T
        turned.append(
            jnp.concatenate([flipped[q * cycles : (q + 1) * cycles] for q in range(4)], axis=1)
        )
    high, low = split(jnp.concatenate(turned, axis=0))
    out = (
        jnp.dot(high, azimuth_ref[0], preferred_element_type=f32)
        + jnp.dot(high, azimuth_ref[1], preferred_element_type=f32)
        + jnp.dot(low, azimuth_ref[0], preferred_element_type=f32)
    )
    for k in range(moments):
        out_ref[k] = out[k * cycles : (k + 1) * cycles]


def params(mib):
    return pltpu.CompilerParams(vmem_limit_bytes=mib << 20)


def local(visibility, beam_blocks, legendre, m_table, mode_counts, moment_weights):
    time_local, modes = visibility.shape[1], visibility.shape[3]
    places = lax.axis_size("chip") * lax.axis_size("core")
    freqs = lax.axis_size("freq")
    total_time = time_local * places
    slots_all = m_table.shape[0]
    slots = slots_all // places
    cycles = legendre.shape[2]
    moments = moment_weights.shape[0]
    depth = 2 * time_local

    other = lax.ppermute(visibility, "core", SWAP)
    beam, degrees = beam_blocks.reshape(2 * slots, modes, -1), beam_blocks.shape[4]
    rows = modes // PIECES
    head, own, mode_mask, degree_mask, table, spread, line = pl.pallas_call(
        functools.partial(prepare_kernel, norm=1.0 / (LIFT * math.sqrt(total_time)), time_local=time_local),
        out_shape=(
            pltpu.VMEM((HEADS, rows, degrees), bf16),
            pltpu.VMEM((depth, modes), bf16),
            pltpu.VMEM((2 * slots, modes), f32),
            pltpu.VMEM((2 * slots, degrees), f32),
            pltpu.VMEM((4 * slots_all, 2 * depth), bf16),
            pltpu.VMEM((moments, freqs, 128), f32),
            pltpu.VMEM((1, slots_all), i32),
        ),
        in_specs=[ANY] * 6,
        out_specs=(VMEM,) * 7,
        scratch_shapes=[
            pltpu.SMEM(m_table.shape, i32),
            pltpu.SMEM(mode_counts.shape, i32),
            pltpu.SMEM(moment_weights.shape, f32),
            pltpu.VMEM((time_local, 2, modes), bf16),
            pltpu.SemaphoreType.DMA((5,)),
            pltpu.SemaphoreType.DMA((HEADS,)),
        ],
        compiler_params=params(54),
        name="prepare",
    )(m_table, mode_counts, moment_weights, m_table[None, :], visibility[0], beam)
    parts = pl.pallas_call(
        transform_kernel,
        out_shape=jax.ShapeDtypeStruct((2 * slots_all, modes // 2), f32),
        in_specs=[VMEM, VMEM, VMEM],
        out_specs=VMEM,
        compiler_params=params(16),
        name="transform",
    )(table, own, other[0])
    parts = lax.all_to_all(
        parts.reshape(places, 2 * slots, modes // 2).astype(f16), ("chip", "core"), split_axis=0, concat_axis=0
    ).astype(f32)
    sums, swapped, azimuth = pl.pallas_call(
        contract_kernel,
        out_shape=(
            pltpu.VMEM((places // 2, 128), f32),
            pltpu.VMEM((places // 2, 128), f32),
            pltpu.VMEM((2, 2 * slots_all, CIRCLE // freqs), bf16),
        ),
        in_specs=[VMEM, VMEM, VMEM, VMEM, VMEM, ANY, ANY],
        out_specs=(VMEM, VMEM, VMEM),
        scratch_shapes=[
            pltpu.VMEM((2 * slots, cycles // 128, 128), f32),
            pltpu.VMEM(beam.shape, bf16),
            pltpu.VMEM(legendre.shape, bf16),
            pltpu.SemaphoreType.DMA((3 * slots * PIECES - HEADS,)),
        ],
        compiler_params=params(48),
        name="contract",
    )(parts, mode_mask, degree_mask, line, head, beam, legendre)
    swapped = lax.ppermute(swapped, "core", SWAP)
    first = lax.axis_index("core") == 0
    pair = jnp.stack(
        [jnp.where(first, sums, swapped), jnp.where(first, swapped, sums)], axis=1
    ).astype(bf16)
    sums = lax.all_to_all(
        jnp.broadcast_to(pair[None], (freqs,) + pair.shape).reshape((-1,) + pair.shape[1:]),
        ("freq", "chip"),
        split_axis=0,
        concat_axis=0,
    ).reshape(freqs * places, 128)
    return pl.pallas_call(
        synthesis_kernel,
        out_shape=jax.ShapeDtypeStruct((moments, cycles // places, CIRCLE // freqs), f32),
        in_specs=[VMEM, VMEM, VMEM],
        out_specs=VMEM,
        compiler_params=params(16),
        name="synthesis",
    )(spread, sums, azimuth)


def solution(mesh):
    freqs, places = mesh.devices.shape
    fine = Mesh(mesh.devices.reshape(freqs, places // 2, 2), ("freq", "chip", "core"))
    ma = ("chip", "core")
    placed = (
        P("freq", ma, None, None),
        P("freq", ma, None, None, None),
        P(ma, None, None),
        P(),
        P(),
        P(),
    )
    return jax.shard_map(
        local, mesh=fine, in_specs=placed, out_specs=P(None, ma, "freq"), check_vma=False
    )
```
